32 devices in a mesh: py: 4 (over y, core), px: 8 (over z, x).
Axes of the slice: x: 2, y: 2, z: 4, core: 2. Of those that a mesh axis runs over, the one named last changes fastest.
Arguments:
- pieces: bfloat16 [2048, 128, 128], P(('py', 'px')), may hold values from -6 to 6
- owner_map: int32 [2048], P(('py', 'px')), may hold values from 0 to 31, as said below
- offsets: int32 [2048], P(('py', 'px')), may hold values from 0 to 63
- template: bfloat16 [4096, 8192], P('py', 'px'), may hold values from -32 to 32
- coefficients: float32 [3, 15], replicated, may hold values from -3 to 3
Outputs:
- difference: float32 [4096, 8192], P('py', 'px')
The draws below stay inside these ranges and needn't reach their ends.
Inputs may be any that keep to these rules, and one draw needn't show every extreme that they name: owner_map[p] is the tile of the device holding p or one of the eight tiles around it inside the grid; no device sends more than 16 pieces to one tile, and every device sends exactly 16 to one of its tiles.
All inputs are finite; a program needn't handle non-finite values.
Results may differ from the reference program's by a relative error of at most 0.0021.
Values may be sent and summed in bfloat16 or wider, within the bound.
No kernel may reach another device: no remote copies, remote signals or barrier semaphores. Data moves between devices by JAX's collectives and lax.ppermute only.
A program may use at most 128 MiB of HBM per device.

```python
import jax
import jax.numpy as jnp
from jax import lax

BLK = 128
HALO = 16
BASES = 3
TERMS = 15
TB = 8
P_DEV = 64
CAP = 16
TILE_ROWS = 4
TILE_COLS = 8
NYP = 4096
NXP = 8192
PIECES = 2048
DEVICES = 32


def draw_owner_map(key, part):
    key_pick, key_score, key_shuffle = jax.random.split(key, 3)
    senders = jnp.arange(DEVICES, dtype=jnp.int32)
    sender_row = senders // TILE_COLS
    sender_col = senders % TILE_COLS
    buckets = jnp.arange(9, dtype=jnp.int32)
    target_row = sender_row[:, None] + (buckets // 3 - 1)[None, :]
    target_col = sender_col[:, None] + (buckets % 3 - 1)[None, :]
    usable = (target_row >= 0) & (target_row < TILE_ROWS) & (target_col >= 0) & (target_col < TILE_COLS)
    picked = jax.random.randint(key_pick, (DEVICES,), 0, 9)
    picked_ok = jnp.take_along_axis(usable, picked[:, None], axis=1)[:, 0]
    forced = jnp.where(picked_ok, picked, 4)
    slot_bucket = jnp.repeat(buckets, CAP)
    slot_ids = jnp.arange(9 * CAP, dtype=jnp.int32)
    scores = jax.random.randint(key_score, (DEVICES, 9 * CAP), 0, 1 << 20) * (9 * CAP) + slot_ids[None, :]
    scores = jnp.where(slot_bucket[None, :] == forced[:, None], slot_ids[None, :] - 9 * CAP, scores)
    scores = jnp.where(usable[:, slot_bucket], scores, (1 << 30) + slot_ids[None, :])
    ranked = jnp.argsort(scores, axis=1)[:, :P_DEV]
    chosen = jnp.take_along_axis(jnp.broadcast_to(slot_bucket[None, :], (DEVICES, 9 * CAP)), ranked, axis=1)
    shuffle_scores = jax.random.randint(key_shuffle, (DEVICES, P_DEV), 0, 1 << 20) * P_DEV + jnp.arange(P_DEV, dtype=jnp.int32)[None, :]
    chosen = jnp.take_along_axis(chosen, jnp.argsort(shuffle_scores, axis=1), axis=1)
    owner_tiles = (sender_row[:, None] + chosen // 3 - 1) * TILE_COLS + sender_col[:, None] + chosen % 3 - 1
    return owner_tiles.reshape(-1).astype(jnp.int32)


def draw_template(key, part):
    first_key, second_key = jax.random.split(key)
    spread = jax.random.truncated_normal(second_key, -4.0, 4.0, (NYP, NXP), jnp.float32)
    rough = jax.random.truncated_normal(first_key, -4.0, 4.0, (NYP, NXP), jnp.float32)
    values = 1.0 + rough * jnp.exp(0.5 * spread)
    return values.astype(jnp.bfloat16)


def place_ends(result, key, least, largest):
    dims = result.shape
    place = [jax.random.randint(jax.random.fold_in(key, axis), (), 0, dims[axis]) for axis in range(len(dims))]
    result = result.at[tuple(place)].set(least)
    longest = dims.index(max(dims))
    place[longest] = (place[longest] + 1) % dims[longest]
    return result.at[tuple(place)].set(largest)


def steps_of(stream_key, extent, cuts, smallest, top_value):
    gain = 1.0
    for axis_at, parts in cuts:
        steps = jax.random.uniform(jax.random.fold_in(jax.random.fold_in(stream_key, 6), axis_at), (parts,), jnp.float32, smallest / len(cuts), top_value / len(cuts))
        gain = gain * jnp.repeat(jnp.exp(steps), extent[axis_at] // parts).reshape((-1,) + (1,) * (len(extent) - 1 - axis_at))
    return gain


def gaussian(rng, dims, width, reach, cuts=(), held_as=jnp.bfloat16):
    values = width * jax.random.normal(rng, dims, jnp.float32)
    if cuts:
        values = values * steps_of(rng, dims, cuts, -0.22, 0.18)
    return jnp.clip(values, -reach, reach).astype(held_as)


def setup_inputs(seed: int = 0) -> dict:
    keys = jax.random.split(jax.random.key(seed), 6)
    pieces = gaussian(keys[0], (PIECES, BLK, BLK), 1.0, 6.0, ((0, 32),))
    owner_map = draw_owner_map(jax.random.fold_in(keys[5], 71), 0)
    offsets = place_ends(jax.random.randint(keys[2], (PIECES,), 0, TB * TB), jax.random.fold_in(keys[2], 1), 0, (TB * TB) - 1).astype(jnp.int32)
    template = draw_template(jax.random.fold_in(keys[5], 71), 0)
    coefficients = gaussian(keys[4], (BASES, TERMS), 0.5, 3.0, (), jnp.float32)
    return {"pieces": pieces, "owner_map": owner_map, "offsets": offsets, "template": template, "coefficients": coefficients}


sigma_fractions = (0.09375, 0.1875, 0.375)
term_powers = [(degree - power_v, power_v) for degree in range(5) for power_v in range(degree + 1)]


def gauss_taps():
    positions = jnp.arange(-HALO, HALO + 1).astype(jnp.float32)
    stacked = []
    for fraction in sigma_fractions:
        sigma = fraction * HALO
        values = jnp.exp(-positions * positions / (2.0 * sigma * sigma))
        stacked.append(values / jnp.sum(values))
    return jnp.stack(stacked).astype(jnp.bfloat16)


def spatial_weight(coef_row, rows_coord, cols_coord):
    rows_pow = [jnp.ones_like(rows_coord)]
    cols_pow = [jnp.ones_like(cols_coord)]
    for degree in range(1, 5):
        rows_pow.append(rows_pow[-1] * rows_coord)
        cols_pow.append(cols_pow[-1] * cols_coord)
    running = jnp.zeros((rows_coord.shape[0], cols_coord.shape[0]), jnp.float32)
    for power_v in range(5):
        inner_sum = jnp.zeros_like(cols_coord)
        for power_u in range(5 - power_v):
            inner_sum = inner_sum + coef_row[term_powers.index((power_u, power_v))] * cols_pow[power_u]
        running = running + rows_pow[power_v][:, None] * inner_sum[None, :]
    return running


def smooth_along(sky_image, weights, axis_pick):
    if axis_pick == 0:
        padded = jnp.pad(sky_image, ((HALO, HALO), (0, 0)))
    else:
        padded = jnp.pad(sky_image, ((0, 0), (HALO, HALO)))
    length = sky_image.shape[axis_pick]

    def add_term(tap_index, running):
        return running + weights[tap_index] * lax.dynamic_slice_in_dim(padded, tap_index, length, axis_pick)

    return lax.fori_loop(0, 2 * HALO + 1, add_term, jnp.zeros_like(sky_image))


def reference(pieces, owner_map, offsets, template, coefficients):
    blocks_across = TILE_COLS * TB
    blocks_down = TILE_ROWS * TB
    block_row = (owner_map // TILE_COLS) * TB + offsets // TB
    block_col = (owner_map % TILE_COLS) * TB + offsets % TB
    block_of = (block_row * blocks_across + block_col).astype(jnp.int32)
    block_sums = jnp.zeros((blocks_down * blocks_across, BLK, BLK), jnp.float32).at[block_of].add(pieces.astype(jnp.float32))
    coverage = jnp.zeros((blocks_down * blocks_across,), jnp.float32).at[block_of].add(1.0)
    science = block_sums / jnp.maximum(coverage, 1.0)[:, None, None]
    science = science.reshape(blocks_down, blocks_across, BLK, BLK).transpose(0, 2, 1, 3).reshape(NYP, NXP)
    taps = gauss_taps().astype(jnp.float32)
    sky_image = template.astype(jnp.float32)
    rows_coord = (jnp.arange(NYP).astype(jnp.float32) + 0.5) * (2.0 / NYP) - 1.0
    cols_coord = (jnp.arange(NXP).astype(jnp.float32) + 0.5) * (2.0 / NXP) - 1.0
    matched = jnp.zeros((NYP, NXP), jnp.float32)
    for basis_index in range(len(sigma_fractions)):
        across = smooth_along(sky_image, taps[basis_index], 1).astype(jnp.bfloat16)
        across = lax.optimization_barrier(across)
        smoothed = smooth_along(across.astype(jnp.float32), taps[basis_index], 0)
        matched = matched + spatial_weight(coefficients[basis_index], rows_coord, cols_coord) * smoothed
    return science - matched
```

```python
import functools

import jax
import jax.numpy as jnp
import ml_dtypes
import numpy as np
from jax import lax
from jax.experimental import pallas as pl
from jax.experimental.pallas import tpu as pltpu
from jax.sharding import PartitionSpec as P

HALO = 16
CAP = 16
BASES = 3
DEGREE = 4
LANES = 128

sigma_fractions = (0.09375, 0.1875, 0.375)
term_powers = [(degree - power_v, power_v) for degree in range(5) for power_v in range(degree + 1)]


def gauss_taps():
    positions = np.arange(-HALO, HALO + 1).astype(np.float32)
    stacked = []
    for fraction in sigma_fractions:
        sigma = fraction * HALO
        values = np.exp(-positions * positions / np.float32(2.0 * sigma * sigma))
        stacked.append(values / np.sum(values))
    return np.stack(stacked).astype(ml_dtypes.bfloat16)


def across_band(taps):
    band = np.zeros((3 * LANES, BASES * LANES), taps.dtype)
    for b in range(BASES):
        for out in range(LANES):
            first = LANES + out - HALO
            band[first : first + 2 * HALO + 1, b * LANES + out] = taps[b]
    return band


def down_band(taps):
    band = np.zeros((BASES, LANES, LANES + 2 * HALO), taps.dtype)
    for b in range(BASES):
        for out in range(LANES):
            band[b, out, out : out + 2 * HALO + 1] = taps[b]
    return band


def order_kernel(cols_total, per_tile, owner_ref, offset_ref, pos_ref, pieces_ref, first_ref, order_ref, code_ref, sem):
    count = owner_ref.shape[0]
    my_row = pos_ref[0]
    my_col = pos_ref[1]
    odd_col = lax.rem(my_col, 2)
    odd_row = lax.rem(my_row, 2)
    near = 1 - 2 * odd_col
    core = 1 - 2 * odd_row

    def steps(p):
        owner = owner_ref[p]
        return owner, lax.div(owner, cols_total) - my_row, lax.rem(owner, cols_total) - my_col

    def one(flag):
        return jnp.where(flag, 1, 0).astype(jnp.int32)

    def counting(p, counts):
        _, dy, dx = steps(p)
        far_diag, far_flat, near_flat = counts
        far = dx == -near
        return (
            far_diag + one(far & (dy != 0)),
            far_flat + one(far & (dy == 0)),
            near_flat + one((dx == near) & (dy == 0)),
        )

    zero = jnp.int32(0)
    far_diag, far_flat, near_flat = lax.fori_loop(0, count, counting, (zero, zero, zero))
    starts = (
        zero,
        far_diag,
        far_diag + far_flat,
        far_diag + far_flat + near_flat,
        zero + (count - 1),
        zero + count,
        zero + count + CAP,
    )
    for slot in range(count, order_ref.shape[0]):
        order_ref[slot] = 0
        code_ref[slot] = -1

    def placing(p, at):
        owner, dy, dx = steps(p)
        a, b, d, e, c, core_at, other_at = at
        flat = dy == 0
        is_far = dx == -near
        is_near = dx == near
        here = dx == 0
        is_a = is_far & (dy != 0)
        is_b = is_far & flat
        is_d = is_near & flat
        is_c = is_near & (dy != 0)
        slot = jnp.where(is_a, a, jnp.where(is_b, b, jnp.where(is_d, d, jnp.where(is_c, c, e))))
        code = owner * per_tile + offset_ref[p]
        order_ref[slot] = p
        code_ref[slot] = code
        to_core = here & (dy == core)
        to_other = here & (dy == -core)

        @pl.when(to_core | to_other)
        def _():
            extra = jnp.where(to_core, core_at, other_at)
            order_ref[extra] = p
            code_ref[extra] = code

        return (
            a + one(is_a),
            b + one(is_b),
            d + one(is_d),
            e + one(here),
            c - one(is_c),
            core_at + one(to_core),
            other_at + one(to_other),
        )

    lax.fori_loop(0, count, placing, starts)
    gather(order_ref, 0, pieces_ref, first_ref, sem)


def gather(order_ref, base, pieces_ref, out_ref, sem):
    def start(slot, carry):
        pltpu.make_async_copy(pieces_ref.at[order_ref[base + slot]], out_ref.at[slot], sem).start()
        return carry

    lax.fori_loop(0, out_ref.shape[0], start, 0)
    pltpu.make_async_copy(out_ref, out_ref, sem).wait()


def gather_kernel(bases, order_ref, pieces_ref, *refs):
    outs, sems = refs[:-1], refs[-1]
    for index, (base, out_ref) in enumerate(zip(bases, outs)):

        def start(slot, carry, base=base, out_ref=out_ref, index=index):
            pltpu.make_async_copy(
                pieces_ref.at[order_ref[base + slot]], out_ref.at[slot], sems.at[index]
            ).start()
            return carry

        lax.fori_loop(0, out_ref.shape[0], start, 0)
    for index, out_ref in enumerate(outs):
        pltpu.make_async_copy(out_ref, out_ref, sems.at[index]).wait()


SMEM = pl.BlockSpec(memory_space=pltpu.SMEM)
VMEM = pl.BlockSpec(memory_space=pltpu.VMEM)
ANY = pl.BlockSpec(memory_space=pl.ANY)


def order_pieces(owner_map, offsets, position, pieces, cols_total, per_tile):
    count, side, _ = pieces.shape
    chunk = jax.ShapeDtypeStruct((CAP, side, side), pieces.dtype)
    table = jax.ShapeDtypeStruct((2 * count,), jnp.int32)
    first, order, codes = pl.pallas_call(
        functools.partial(order_kernel, cols_total, per_tile),
        out_shape=(chunk, table, table),
        in_specs=[SMEM, SMEM, SMEM, ANY],
        out_specs=(ANY, SMEM, SMEM),
        scratch_shapes=[pltpu.SemaphoreType.DMA],
        name="order_pieces",
    )(owner_map, offsets, position, pieces)
    bases = tuple(range(CAP, count + 2 * CAP, CAP))
    rest = pl.pallas_call(
        functools.partial(gather_kernel, bases),
        out_shape=(chunk,) * len(bases),
        in_specs=[SMEM, ANY],
        out_specs=(ANY,) * len(bases),
        scratch_shapes=[pltpu.SemaphoreType.DMA((len(bases),))],
        name="gather_pieces",
    )(order, pieces)
    chunks = (first,) + tuple(rest[: count // CAP - 1])
    return chunks, rest[-2], rest[-1], codes


def matched_kernel(
    extent, coef_ref, pos_ref, centre_ref, top_ref, bottom_ref, left_ref, right_ref, across_ref, down_ref, out_ref,
    padded, across, polys,
):
    side = centre_ref.shape[0]
    tall = side + 2 * HALO
    rows_total, cols_total = extent
    padded[:, :LANES] = left_ref[...]
    padded[:, LANES + side :] = right_ref[...]
    padded[:HALO, LANES : LANES + side] = top_ref[...]
    padded[HALO + side :, LANES : LANES + side] = bottom_ref[...]
    padded[HALO : HALO + side, LANES : LANES + side] = centre_ref[...]

    col = lax.broadcasted_iota(jnp.int32, (1, side), 1) + pos_ref[1] * side
    u = (col.astype(jnp.float32) + 0.5) * (2.0 / (side * cols_total)) - 1.0
    powers = [jnp.ones_like(u)]
    for _ in range(DEGREE):
        powers.append(powers[-1] * u)
    for b in range(BASES):
        for j in range(DEGREE + 1):
            total = jnp.zeros_like(u)
            for i in range(DEGREE + 1 - j):
                total = total + coef_ref[b, term_powers.index((i, j))] * powers[i]
            polys[b * (DEGREE + 1) + j : b * (DEGREE + 1) + j + 1, :] = total

    def across_rows(start, rows):
        for j in range(side // LANES):
            window = padded[pl.ds(start, rows), j * LANES : (j + 3) * LANES]
            summed = jnp.dot(window, across_ref[...], preferred_element_type=jnp.float32)
            for b in range(BASES):
                across[b, pl.ds(start, rows), j * LANES : (j + 1) * LANES] = summed[
                    :, b * LANES : (b + 1) * LANES
                ].astype(jnp.bfloat16)

    def across_step(step, carry):
        across_rows(pl.multiple_of(step * LANES, LANES), LANES)
        return carry

    lax.fori_loop(0, side // LANES, across_step, 0)
    across_rows(side, tall - side)

    wide = 256

    def down_step(step, carry):
        start = pl.multiple_of(step * LANES, LANES)
        row = lax.broadcasted_iota(jnp.int32, (LANES, wide), 0) + start + pos_ref[0] * side
        v = (row.astype(jnp.float32) + 0.5) * (2.0 / (side * rows_total)) - 1.0
        for n in range(side // wide):
            cols = slice(n * wide, (n + 1) * wide)
            total = jnp.zeros((LANES, wide), jnp.float32)
            for b in range(BASES):
                smoothed = jnp.dot(
                    down_ref[b], across[b, pl.ds(start, LANES + 2 * HALO), cols], preferred_element_type=jnp.float32
                )
                first = b * (DEGREE + 1)
                weight = polys[first + DEGREE : first + DEGREE + 1, cols] * v
                for j in range(DEGREE - 1, 0, -1):
                    weight = (weight + polys[first + j : first + j + 1, cols]) * v
                weight = weight + polys[first : first + 1, cols]
                total = total + weight * smoothed
            out_ref[pl.ds(start, LANES), cols] = -total
        return carry

    lax.fori_loop(0, side // LANES, down_step, 0)


def minus_matched(extent, coefficients, position, centre, top, bottom, left, right):
    side = centre.shape[0]
    tall = side + 2 * HALO
    taps = gauss_taps()
    return pl.pallas_call(
        functools.partial(matched_kernel, extent),
        out_shape=jax.ShapeDtypeStruct((side, side), jnp.float32),
        in_specs=[SMEM, SMEM] + [VMEM] * 7,
        out_specs=VMEM,
        scratch_shapes=[
            pltpu.VMEM((tall, side + 2 * LANES), jnp.bfloat16),
            pltpu.VMEM((BASES, tall, side), jnp.bfloat16),
            pltpu.VMEM((16, side), jnp.float32),
        ],
        compiler_params=pltpu.CompilerParams(vmem_limit_bytes=40 << 20),
        cost_estimate=pl.CostEstimate(flops=8 << 30, bytes_accessed=8 << 20, transcendentals=0),
        name="matched_template",
    )(
        coefficients, position, centre, top, bottom, left, right,
        jnp.asarray(across_band(taps)), jnp.asarray(down_band(taps)),
    )


def add_kernel(plan, per_tile, blocks_side, pos_ref, codes_ref, share_ref, base_ref, *refs):
    count = len(plan)
    messages, out_ref, held, sems = refs[:count], refs[count], refs[count + 1], refs[count + 2]
    side = held.shape[0]
    fetch = pltpu.make_async_copy(base_ref, held, sems.at[0])
    fetch.start()
    fetch.wait()
    mine = pos_ref[2]
    block_side = side // blocks_side
    for message, (source, first) in zip(messages, plan):

        def visit(slot, carry, message=message, source=source, first=first):
            code = codes_ref[source, first + slot]
            block = code - mine * per_tile

            @pl.when((block >= 0) & (block < per_tile))
            def _():
                rows = pl.ds(pl.multiple_of(lax.div(block, blocks_side) * block_side, block_side), block_side)
                cols = pl.ds(pl.multiple_of(lax.rem(block, blocks_side) * block_side, block_side), block_side)
                held[rows, cols] = held[rows, cols] + message[slot].astype(jnp.float32) * share_ref[block]

            return carry

        lax.fori_loop(0, message.shape[0], visit, 0)
    store = pltpu.make_async_copy(held, out_ref, sems.at[1])
    store.start()
    store.wait()


def add_pieces(name, base, position, codes, shares, messages, blocks_side, cost):
    side = base.shape[0]
    plan = tuple((source, first) for _, source, first in messages)
    arrays = [array for array, _, _ in messages]
    return pl.pallas_call(
        functools.partial(add_kernel, plan, blocks_side * blocks_side, blocks_side),
        out_shape=jax.ShapeDtypeStruct(base.shape, base.dtype),
        in_specs=[SMEM, SMEM, SMEM, ANY] + [VMEM] * len(arrays),
        out_specs=ANY,
        scratch_shapes=[pltpu.VMEM((side, side), jnp.float32), pltpu.SemaphoreType.DMA((2,))],
        input_output_aliases={3: 0},
        compiler_params=pltpu.CompilerParams(vmem_limit_bytes=40 << 20),
        cost_estimate=pl.CostEstimate(flops=cost, bytes_accessed=8 << 20, transcendentals=0),
        name=name,
    )(position, codes, shares, base, *arrays)


class Grid:
    def __init__(self, rows, cols):
        self.rows, self.cols = rows, cols

    def pairs(self, target):
        found = []
        for row in range(self.rows):
            for col in range(self.cols):
                to_row, to_col = target(row, col)
                if 0 <= to_row < self.rows and 0 <= to_col < self.cols:
                    found.append((row * self.cols + col, to_row * self.cols + to_col))
        return found

    def near(self, array):
        return lax.ppermute(array, ("py", "px"), self.pairs(lambda r, c: (r, c ^ 1)))

    def far(self, array):
        return lax.ppermute(array, ("py", "px"), self.pairs(lambda r, c: (r, c + 1 if c % 2 else c - 1)))

    def beyond(self, array):
        return lax.ppermute(array, ("py", "px"), self.pairs(lambda r, c: (r, c - 2 if c % 2 else c + 2)))

    def core(self, array):
        return lax.ppermute(array, ("py", "px"), self.pairs(lambda r, c: (r ^ 1, c)))

    def other(self, array):
        return lax.ppermute(array, ("py", "px"), self.pairs(lambda r, c: (r + 1 if r % 2 else r - 1, c)))


def on_device(pieces, owner_map, offsets, template, coefficients):
    bar = lax.optimization_barrier
    rows_total = lax.axis_size("py")
    cols_total = lax.axis_size("px")
    grid = Grid(rows_total, cols_total)
    my_row = lax.axis_index("py")
    my_col = lax.axis_index("px")
    position = jnp.stack([my_row, my_col, my_row * cols_total + my_col]).astype(jnp.int32)
    even_row = my_row % 2 == 0
    even_col = my_col % 2 == 0
    count, block_side, _ = pieces.shape
    side = template.shape[0]
    blocks_side = side // block_side
    per_tile = blocks_side * blocks_side

    chunks, own_core, own_other, codes = order_pieces(owner_map, offsets, position, pieces, cols_total, per_tile)

    left_strip = template[:, :HALO].T
    right_strip = template[:, side - HALO :].T
    near_strip = grid.near(jnp.where(even_col, right_strip, left_strip))
    far_strip = grid.far(jnp.where(even_col, left_strip, right_strip))

    near_parts = [grid.near(chunk) for chunk in chunks]
    far_parts = [grid.beyond(part) for part in near_parts[:-1]]
    own_from = (grid.core(own_core), grid.other(own_other))

    top_rows = jnp.concatenate([template[:HALO], near_strip[:, :HALO], far_strip[:, :HALO]], axis=1)
    low = side - HALO
    low_rows = jnp.concatenate([template[low:], near_strip[:, low:], far_strip[:, low:]], axis=1)
    core_rows = grid.core(jnp.where(even_row, low_rows, top_rows))
    other_rows = grid.other(jnp.where(even_row, top_rows, low_rows))
    above = jnp.where(even_row, other_rows, core_rows)
    below = jnp.where(even_row, core_rows, other_rows)
    near_full = jnp.concatenate([above[:, side : side + HALO], near_strip, below[:, side : side + HALO]], axis=1)
    far_full = jnp.concatenate([above[:, side + HALO :], far_strip, below[:, side + HALO :]], axis=1)
    left = jnp.where(even_col, far_full, near_full).T
    right = jnp.where(even_col, near_full, far_full).T
    left = jnp.pad(left, ((0, 0), (LANES - HALO, 0)))
    right = jnp.pad(right, ((0, 0), (0, LANES - HALO)))
    base = minus_matched(
        (rows_total, cols_total), coefficients, position, template, above[:, :side], below[:, :side], left, right
    )

    everyone = lax.all_gather(codes, ("py", "px"))
    near_col = my_col + jnp.where(even_col, 1, -1)
    far_col = my_col - jnp.where(even_col, 1, -1)
    core_row = my_row + jnp.where(even_row, 1, -1)
    other_row = my_row - jnp.where(even_row, 1, -1)
    cols9 = jnp.stack([my_col, near_col, far_col] * 3)
    rows9 = jnp.repeat(jnp.stack([my_row, core_row, other_row]), 3)
    inside = (cols9 >= 0) & (cols9 < cols_total) & (rows9 >= 0) & (rows9 < rows_total)
    around = everyone[jnp.where(inside, rows9 * cols_total + cols9, 0)]
    around = jnp.where(inside[:, None], around, -1)
    blocks = around[:, :count].reshape(-1) - position[2] * per_tile
    coverage = jnp.sum(
        (blocks[:, None] == jnp.arange(per_tile, dtype=jnp.int32)[None, :]).astype(jnp.float32), axis=0
    )
    shares = 1.0 / jnp.maximum(coverage, 1.0)

    own, near, far = 0, 1, 2
    core, other = 3, 6
    early = [(chunk, own, i * CAP) for i, chunk in enumerate(chunks)]
    early += [(own_from[0], core, count), (own_from[1], other, count + CAP)]
    early += [(part, near, i * CAP) for i, part in enumerate(near_parts[:2])]
    early += [(far_parts[0], far, 0)]
    base = add_pieces("add_early", base, position, around, shares, early, blocks_side, 2 << 30)

    late = [(near_parts[2], near, 2 * CAP), (far_parts[1], far, CAP)]
    last = []
    for index in (0, 1):
        (late if index == 0 else last).extend(
            [
                (grid.core(far_parts[index]), core + far, index * CAP),
                (grid.other(far_parts[index]), other + far, index * CAP),
            ]
        )
    base = add_pieces("add_late", base, position, around, shares, late, blocks_side, 2 << 30)
    last += [(near_parts[3], near, 3 * CAP), (far_parts[2], far, 2 * CAP)]
    for index in (2, 3):
        last.extend(
            [
                (grid.core(near_parts[index]), core + near, index * CAP),
                (grid.other(near_parts[index]), other + near, index * CAP),
            ]
        )
    return add_pieces("add_last", base, position, around, shares, last, blocks_side, 2 << 30)


def solution(mesh):
    in_specs = (P(("py", "px"), None, None), P(("py", "px")), P(("py", "px")), P("py", "px"), P())
    out_specs = P("py", "px")
    return jax.shard_map(on_device, mesh=mesh, in_specs=in_specs, out_specs=out_specs, check_vma=False)
```

```python
import functools

import jax
import jax.numpy as jnp
import ml_dtypes
import numpy as np
from jax import lax
from jax.experimental import pallas as pl
from jax.experimental.pallas import tpu as pltpu
from jax.sharding import PartitionSpec as P

HALO = 16
CAP = 16
BASES = 3
DEGREE = 4
LANES = 128

sigma_fractions = (0.09375, 0.1875, 0.375)
term_powers = [(degree - power_v, power_v) for degree in range(5) for power_v in range(degree + 1)]


def gauss_taps():
    positions = np.arange(-HALO, HALO + 1).astype(np.float32)
    stacked = []
    for fraction in sigma_fractions:
        sigma = fraction * HALO
        values = np.exp(-positions * positions / np.float32(2.0 * sigma * sigma))
        stacked.append(values / np.sum(values))
    return np.stack(stacked).astype(ml_dtypes.bfloat16)


def across_band(taps):
    band = np.zeros((2 * LANES, BASES * LANES), taps.dtype)
    for b in range(BASES):
        for out in range(LANES):
            band[out : out + 2 * HALO + 1, b * LANES + out] = taps[b]
    return band


def down_band(taps):
    band = np.zeros((BASES, LANES, LANES + 2 * HALO), taps.dtype)
    for b in range(BASES):
        for out in range(LANES):
            band[b, out, out : out + 2 * HALO + 1] = taps[b]
    return band


SMEM = pl.BlockSpec(memory_space=pltpu.SMEM)
VMEM = pl.BlockSpec(memory_space=pltpu.VMEM)
ANY = pl.BlockSpec(memory_space=pl.ANY)
CHEAP = pl.CostEstimate(flops=0, bytes_accessed=0, transcendentals=0)


def split_index(index, size):
    if size & (size - 1) == 0:
        return jnp.right_shift(index, size.bit_length() - 1), jnp.bitwise_and(index, size - 1)
    return lax.div(index, size), lax.rem(index, size)


def piece_at(message, slot, block_side):
    if len(message.shape) == 3:
        return message.at[slot]
    start = slot * block_side
    if not isinstance(slot, int):
        start = pl.multiple_of(start, block_side)
    return message.at[pl.ds(start, block_side), :]


def order_kernel(cols_total, owner_ref, offset_ref, pos_ref, pieces_ref, template_ref, *refs):
    outs = refs[:-9]
    near_ref, far_ref, label_ref, held, edges, meta, order_v, order_s, sems = refs[-9:]
    count = held.shape[0]
    fetch = pltpu.make_async_copy(pieces_ref, held, sems.at[len(outs)])
    fetch.start()
    side = edges.shape[1]
    rims = [
        pltpu.make_async_copy(template_ref.at[:, :LANES], edges.at[0], sems.at[len(outs) + 2]),
        pltpu.make_async_copy(template_ref.at[:, side - LANES :], edges.at[1], sems.at[len(outs) + 3]),
    ]
    for rim in rims:
        rim.start()
    my_row, my_col = pos_ref[0], pos_ref[1]
    even_col = jnp.bitwise_and(my_col, 1) == 0
    near = 1 - 2 * jnp.bitwise_and(my_col, 1)
    core = 1 - 2 * jnp.bitwise_and(my_row, 1)

    meta[...] = jnp.zeros_like(meta)
    meta[0:1, :count] = owner_ref[...]
    meta[1:2, :count] = offset_ref[...]
    lane = lax.broadcasted_iota(jnp.int32, (1, LANES), 1)
    row, col = split_index(meta[0:1, :], cols_total)
    dy, dx = row - my_row, col - my_col
    flat = dy == 0
    to_core = dy == core
    kind = jnp.where(
        dx == 0,
        jnp.where(flat, 4, jnp.where(to_core, 5, 6)),
        jnp.where(
            dx == near,
            jnp.where(flat, 3, jnp.where(to_core, 8, 7)),
            jnp.where(flat, 2, jnp.where(to_core, 1, 0)),
        ),
    )
    kind = jnp.where(lane < count, kind, 9)
    packed = (3 * (dy + 1) + dx + 2) * 256 + meta[1:2, :]

    def both(line):
        across = jnp.broadcast_to(line.astype(jnp.float32), (LANES, LANES))
        return across, across.T

    kind_l, kind_s = both(kind)
    _, packed_s = both(packed)
    sub = lax.broadcasted_iota(jnp.int32, (LANES, LANES), 0)
    lan = lax.broadcasted_iota(jnp.int32, (LANES, LANES), 1)

    def total(flags):
        return jnp.sum(jnp.where(flags, 1.0, 0.0), axis=1, keepdims=True)

    rank = total((kind_l == kind_s) & (lan < sub))
    mine = kind_s[:, 0:1]
    before = total((kind_l < kind_s) & ((kind_l >= 7.0) | (kind_s < 7.0)))
    slot = jnp.where(mine < 7.0, before + rank, jnp.where(mine < 9.0, (count - 1.0) - before - rank, -1.0))
    extra = jnp.where(
        mine == 5.0, count + rank, jnp.where(mine == 6.0, (count + CAP) + rank, -1.0)
    )
    place = lan.astype(jnp.float32)
    here = (place == slot) | (place == extra)
    order = jnp.sum(jnp.where(here, sub.astype(jnp.float32), 0.0), axis=0, keepdims=True)
    labels = jnp.sum(jnp.where(here, packed_s, 0.0), axis=0, keepdims=True)
    order_v[...] = jnp.broadcast_to(order, order_v.shape).astype(jnp.int32)
    to_smem = pltpu.make_async_copy(order_v, order_s, sems.at[len(outs) + 1])
    to_smem.start()
    labels = labels.astype(jnp.int32)
    which = lax.broadcasted_iota(jnp.int32, label_ref.shape, 0)
    label_rows = jnp.where(
        which == 0, jnp.right_shift(labels, 8), jnp.where(which == 1, jnp.bitwise_and(labels, 255), 0)
    ).astype(jnp.float32).astype(jnp.bfloat16)
    label_ref[...] = label_rows
    near_ref[:, side:] = label_rows
    far_ref[:, side:] = label_rows
    to_smem.wait()
    fetch.wait()
    for index, out_ref in enumerate(outs):
        for slot_at in range(CAP):
            pltpu.make_async_copy(
                held.at[order_s[0, index * CAP + slot_at]], piece_at(out_ref, slot_at, held.shape[1]), sems.at[index]
            ).start()
    for rim in rims:
        rim.wait()
    for block in range(side // LANES):
        rows = slice(block * LANES, (block + 1) * LANES)
        left = edges[0, rows, :].astype(jnp.float32).T[:HALO]
        right = edges[1, rows, :].astype(jnp.float32).T[LANES - HALO :]
        near_ref[:, rows] = jnp.where(even_col, right, left).astype(near_ref.dtype)
        far_ref[:, rows] = jnp.where(even_col, left, right).astype(far_ref.dtype)
    for index, out_ref in enumerate(outs):
        pltpu.make_async_copy(outs[0], outs[0], sems.at[index]).wait()


def order_pieces(owner_map, offsets, position, pieces, template, cols_total):
    count, block_side, _ = pieces.shape
    side = template.shape[0]
    parts = count // CAP + 2
    chunk = jax.ShapeDtypeStruct((CAP, block_side, block_side), pieces.dtype)
    mail = chunk
    rim = jax.ShapeDtypeStruct((HALO, side + LANES), template.dtype)
    *outs, near, far, labels = pl.pallas_call(
        functools.partial(order_kernel, cols_total),
        out_shape=(chunk,) * (parts - 2)
        + (mail, mail)
        + (rim, rim, jax.ShapeDtypeStruct((HALO, LANES), template.dtype)),
        in_specs=[VMEM, VMEM, SMEM, ANY, ANY],
        out_specs=(ANY,) * parts + (VMEM,) * 3,
        scratch_shapes=[
            pltpu.VMEM(pieces.shape, pieces.dtype),
            pltpu.VMEM((2, side, LANES), template.dtype),
            pltpu.VMEM((8, LANES), jnp.int32),
            pltpu.VMEM((8, LANES), jnp.int32),
            pltpu.SMEM((8, LANES), jnp.int32),
            pltpu.SemaphoreType.DMA((parts + 4,)),
        ],
        compiler_params=pltpu.CompilerParams(vmem_limit_bytes=58 << 20),
        cost_estimate=CHEAP,
        name="order_pieces",
    )(owner_map.reshape(1, -1), offsets.reshape(1, -1), position, pieces, template)
    return outs[:-2], outs[-2], outs[-1], near, far, labels


def rim_rows(side):
    return HALO * (side // LANES + 3)


def row_rims_kernel(
    pos_ref, template_ref, near_ref, far_ref, label_ref, core_out, other_out, edges, packed, sems
):
    side = edges.shape[2]
    tiles = side // LANES
    fetches = [
        pltpu.make_async_copy(template_ref.at[:HALO, :], edges.at[0], sems.at[0]),
        pltpu.make_async_copy(template_ref.at[side - HALO :, :], edges.at[1], sems.at[1]),
    ]
    for fetch in fetches:
        fetch.start()
    even_row = jnp.bitwise_and(pos_ref[0], 1) == 0
    sub = lax.broadcasted_iota(jnp.int32, (HALO, LANES), 0)
    own = label_ref[...].astype(jnp.float32)
    near = near_ref[:, side:].astype(jnp.float32)
    far = far_ref[:, side:].astype(jnp.float32)
    pairs = own
    for index, table in ((1, near), (2, far)):
        for row in (0, 1):
            pairs = jnp.where(sub == 2 * index + row, table[row : row + 1, :], pairs)
    pairs = pairs.astype(label_ref.dtype)
    corners = []
    for strip in (near_ref, far_ref):
        low = strip[:, side - LANES : side].astype(jnp.float32)
        low = jnp.concatenate([low[:, LANES - HALO :], low[:, : LANES - HALO]], axis=1).astype(strip.dtype)
        corners.append((strip[:, :LANES], low))
    for fetch in fetches:
        fetch.wait()
    stores = []
    for index, (out_ref, upper) in enumerate(((core_out, jnp.logical_not(even_row)), (other_out, even_row))):
        for tile in range(tiles):
            cols = slice(tile * LANES, (tile + 1) * LANES)
            packed[index, tile * HALO : (tile + 1) * HALO, :] = jnp.where(upper, edges[0, :, cols], edges[1, :, cols])
        for corner, (top, low) in enumerate(corners):
            start = (tiles + corner) * HALO
            packed[index, start : start + HALO, :] = jnp.where(upper, top, low)
        packed[index, (tiles + 2) * HALO :, :] = pairs
        rows = out_ref.shape[0]
        stores.append(
            pltpu.make_async_copy(
                packed.at[index], out_ref.at[rows - packed.shape[1] : rows, :], sems.at[2 + index]
            )
        )
        stores[-1].start()
    for store in stores:
        store.wait()


def row_rims(position, template, near, far, labels):
    side = template.shape[0]
    message = jax.ShapeDtypeStruct((rim_rows(side), LANES), template.dtype)
    return pl.pallas_call(
        row_rims_kernel,
        out_shape=(message, message),
        in_specs=[SMEM, ANY, VMEM, VMEM, VMEM],
        out_specs=(ANY, ANY),
        scratch_shapes=[
            pltpu.VMEM((2, HALO, side), template.dtype),
            pltpu.VMEM((2, rim_rows(side), LANES), template.dtype),
            pltpu.SemaphoreType.DMA((4,)),
        ],
        compiler_params=pltpu.CompilerParams(vmem_limit_bytes=58 << 20),
        cost_estimate=CHEAP,
        name="row_rims",
    )(position, template, near, far, labels)


def fill_tables(even_row, even_col, own_ref, core_ref, other_ref, blocks_ref, share_ref):
    near_step = jnp.where(even_col, 1, -1)
    core_step = jnp.where(even_row, 1, -1)
    sub = lax.broadcasted_iota(jnp.int32, (LANES, LANES), 0)
    lane = lax.broadcasted_iota(jnp.int32, (LANES, LANES), 1)
    table = jnp.full((LANES, LANES), -1.0, jnp.float32)
    for group, (ref, row_step) in enumerate(((own_ref, 0), (core_ref, core_step), (other_ref, -core_step))):
        rows = ref[ref.shape[0] - HALO :, :].astype(jnp.float32)
        for index, col_step in enumerate((0, near_step, -near_step)):
            wanted = (5 - 3 * row_step - col_step) * jnp.int32(1)
            match = rows[2 * index : 2 * index + 1, :] == wanted.astype(jnp.float32)
            line = jnp.where(match, rows[2 * index + 1 : 2 * index + 2, :], -1.0)
            table = jnp.where(sub == 3 * group + index, line, table)
    blocks_ref[...] = table[: blocks_ref.shape[0]].astype(jnp.int32)
    upright = table.T
    counts = jnp.zeros((1, LANES), jnp.float32)
    for source in range(9):
        column = upright[: LANES // 2, source : source + 1]
        counts = counts + jnp.sum(
            jnp.where(column == lane[: LANES // 2].astype(jnp.float32), 1.0, 0.0), axis=0, keepdims=True
        )
    share_ref[...] = jnp.broadcast_to(1.0 / jnp.maximum(counts, 1.0), share_ref.shape)


def weight_rows(coef_ref, start, width, side, cols_total, my_col):
    col = lax.broadcasted_iota(jnp.int32, (1, width), 1) + (start + my_col * side)
    u = (col.astype(jnp.float32) + 0.5) * (2.0 / (side * cols_total)) - 1.0
    powers = [jnp.ones_like(u)]
    for _ in range(DEGREE):
        powers.append(powers[-1] * u)
    rows = []
    for b in range(BASES):
        for j in range(DEGREE + 1):
            total = jnp.zeros_like(u)
            for i in range(DEGREE + 1 - j):
                total = total + coef_ref[b, term_powers.index((i, j))] * powers[i]
            rows.append(total)
    return rows


def minus_weighted(smoothed, polys, cols, start, side, rows_total, my_row):
    shape = smoothed[0].shape
    row = lax.broadcasted_iota(jnp.int32, shape, 0) + (start + my_row * side)
    v = (row.astype(jnp.float32) + 0.5) * (2.0 / (side * rows_total)) - 1.0
    total = jnp.zeros(shape, jnp.float32)
    for b in range(BASES):
        power = b * (DEGREE + 1)
        weight = polys[power + DEGREE : power + DEGREE + 1, cols] * v
        for j in range(DEGREE - 1, 0, -1):
            weight = (weight + polys[power + j : power + j + 1, cols]) * v
        weight = weight + polys[power : power + 1, cols]
        total = total - weight * smoothed[b]
    return total


def interior_kernel(
    extent, coef_ref, pos_ref, centre_ref, across_ref, down_ref, out_ref, padded, across, polys, ready, sems
):
    side = centre_ref.shape[0]
    rows_total, cols_total = extent
    inner = side - 2 * LANES
    reach = inner + LANES
    padded[:, :reach] = centre_ref[:, LANES - HALO : LANES - HALO + reach]
    for index, line in enumerate(weight_rows(coef_ref, LANES, inner, side, cols_total, pos_ref[1])):
        polys[index : index + 1, :] = line
    for b in range(BASES):
        across[b, :HALO, :] = jnp.zeros((HALO, inner), across.dtype)
        across[b, HALO + side :, :] = jnp.zeros((HALO, inner), across.dtype)

    tall = side // 2
    for start in (0, tall):
        for j in range(inner // LANES):
            window = padded[start : start + tall, j * LANES : (j + 2) * LANES]
            summed = jnp.dot(window, across_ref[...], preferred_element_type=jnp.float32)
            for b in range(BASES):
                across[b, HALO + start : HALO + start + tall, j * LANES : (j + 1) * LANES] = summed[
                    :, b * LANES : (b + 1) * LANES
                ].astype(across.dtype)

    wide = 256

    def send(start, slot):
        return pltpu.make_async_copy(
            ready.at[slot], out_ref.at[pl.ds(start, LANES), LANES : LANES + inner], sems.at[slot]
        )

    def down_step(step, carry):
        start = pl.multiple_of(step * LANES, LANES)
        slot = jnp.bitwise_and(step, 1)

        @pl.when(step >= 2)
        def _():
            send(start, slot).wait()

        for n in range(inner // wide):
            cols = slice(n * wide, (n + 1) * wide)
            smoothed = [
                jnp.dot(
                    down_ref[b], across[b, pl.ds(start, LANES + 2 * HALO), cols], preferred_element_type=jnp.float32
                )
                for b in range(BASES)
            ]
            ready[slot, :, cols] = minus_weighted(smoothed, polys, cols, start, side, rows_total, pos_ref[0])
        send(start, slot).start()
        return carry

    lax.fori_loop(0, side // LANES, down_step, 0)
    for slot in (0, 1):
        send(0, slot).wait()


def interior(extent, coefficients, position, centre):
    side = centre.shape[0]
    inner = side - 2 * LANES
    taps = gauss_taps()
    return pl.pallas_call(
        functools.partial(interior_kernel, extent),
        out_shape=jax.ShapeDtypeStruct((side, side), jnp.float32),
        in_specs=[SMEM, SMEM] + [VMEM] * 3,
        out_specs=ANY,
        scratch_shapes=[
            pltpu.VMEM((side, inner + LANES), jnp.bfloat16),
            pltpu.VMEM((BASES, side + 2 * HALO, inner), jnp.bfloat16),
            pltpu.VMEM((16, inner), jnp.float32),
            pltpu.VMEM((2, LANES, inner), jnp.float32),
            pltpu.SemaphoreType.DMA((2,)),
        ],
        compiler_params=pltpu.CompilerParams(vmem_limit_bytes=58 << 20),
        cost_estimate=pl.CostEstimate(flops=int(8e9), bytes_accessed=1, transcendentals=0),
        name="matched_inside",
    )(coefficients, position, centre, jnp.asarray(across_band(taps)), jnp.asarray(down_band(taps)))


def frame_kernel(
    extent, coef_ref, pos_ref, near_ref, far_ref, core_ref, other_ref, sent_ref, across_ref, down_ref, template_ref,
    base_ref, out_ref, blocks_ref, share_ref, sides, ends, rims, padded, across, polys, columns, lines, sems,
):
    side = template_ref.shape[0]
    rows_total, cols_total = extent
    deep = 3 * HALO
    inner = side - 2 * LANES
    fetches = [
        pltpu.make_async_copy(template_ref.at[:, : 2 * LANES], sides.at[0], sems.at[0]),
        pltpu.make_async_copy(template_ref.at[:, side - 2 * LANES :], sides.at[1], sems.at[1]),
        pltpu.make_async_copy(template_ref.at[: 2 * HALO, :], ends.at[0], sems.at[2]),
        pltpu.make_async_copy(template_ref.at[side - 2 * HALO :, :], ends.at[1], sems.at[3]),
    ]
    rim_fetches = []
    for index, ref in enumerate((sent_ref, core_ref, other_ref)):
        rows = ref.shape[0]
        rim_fetches.append(
            pltpu.make_async_copy(ref.at[rows - rims.shape[1] : rows, :], rims.at[index], sems.at[4 + index])
        )
    for fetch in rim_fetches + fetches:
        fetch.start()
    even_row = jnp.bitwise_and(pos_ref[0], 1) == 0
    even_col = jnp.bitwise_and(pos_ref[1], 1) == 0
    for fetch in rim_fetches:
        fetch.wait()
    fill_tables(even_row, even_col, rims.at[0], rims.at[1], rims.at[2], blocks_ref, share_ref)
    core_rim, other_rim = rims[1], rims[2]
    tiles = side // LANES

    def lines_of(rim):
        return jnp.concatenate([rim[tile * HALO : (tile + 1) * HALO] for tile in range(tiles)], axis=1)
    for start, first in ((0, 0), (side - LANES, LANES)):
        for index, line in enumerate(weight_rows(coef_ref, start, LANES, side, cols_total, pos_ref[1])):
            polys[index : index + 1, first : first + LANES] = line

    def upright(near_block, far_block, start, rows):
        near_block = near_block.astype(jnp.float32)
        far_block = far_block.astype(jnp.float32)
        empty = jnp.zeros((LANES - HALO, LANES), jnp.float32)
        left = jnp.concatenate([jnp.where(even_col, far_block, near_block), empty], axis=0).T
        right = jnp.concatenate([jnp.where(even_col, near_block, far_block), empty], axis=0).T
        padded[0, start : start + rows, :HALO] = left[:rows, :HALO].astype(padded.dtype)
        padded[1, start : start + rows, LANES + HALO :] = right[:rows, : LANES - HALO].astype(padded.dtype)

    for block in range(side // LANES):
        cols = slice(block * LANES, (block + 1) * LANES)
        upright(near_ref[:, cols], far_ref[:, cols], HALO + block * LANES, LANES)
    near_corner = slice(tiles * HALO, (tiles + 1) * HALO)
    far_corner = slice((tiles + 1) * HALO, (tiles + 2) * HALO)
    for upper, start in ((even_row, 0), (jnp.logical_not(even_row), HALO + side)):
        upright(
            jnp.where(upper, other_rim[near_corner], core_rim[near_corner]),
            jnp.where(upper, other_rim[far_corner], core_rim[far_corner]),
            start,
            HALO,
        )
    above = lines_of(jnp.where(even_row, other_rim, core_rim))
    below = lines_of(jnp.where(even_row, core_rim, other_rim))
    for fetch in fetches:
        fetch.wait()
    reach = 2 * LANES - HALO
    padded[0, HALO : HALO + side, HALO:] = sides[0, :, :reach]
    padded[0, :HALO, HALO:] = above[:, :reach]
    padded[0, HALO + side :, HALO:] = below[:, :reach]
    padded[1, HALO : HALO + side, : LANES + HALO] = sides[1, :, LANES - HALO :]
    padded[1, :HALO, : LANES + HALO] = above[:, side - LANES - HALO :]
    padded[1, HALO + side :, : LANES + HALO] = below[:, side - LANES - HALO :]

    tall = side // 2 + HALO
    for end in (0, 1):
        for start in (0, tall):
            summed = jnp.dot(padded[end, start : start + tall, :], across_ref[...], preferred_element_type=jnp.float32)
            for b in range(BASES):
                across[b, start : start + tall, end * LANES : (end + 1) * LANES] = summed[
                    :, b * LANES : (b + 1) * LANES
                ].astype(across.dtype)
    both = slice(0, 2 * LANES)

    def down_step(step, carry):
        start = pl.multiple_of(step * LANES, LANES)
        smoothed = [
            jnp.dot(down_ref[b], across[b, pl.ds(start, LANES + 2 * HALO), :], preferred_element_type=jnp.float32)
            for b in range(BASES)
        ]
        columns[pl.ds(start, LANES), :] = minus_weighted(smoothed, polys, both, start, side, rows_total, pos_ref[0])
        return carry

    lax.fori_loop(0, side // LANES, down_step, 0)
    stores = [
        pltpu.make_async_copy(columns.at[:, :LANES], out_ref.at[:, :LANES], sems.at[0]),
        pltpu.make_async_copy(columns.at[:, LANES:], out_ref.at[:, side - LANES :], sems.at[1]),
    ]
    for store in stores:
        store.start()

    for index, line in enumerate(weight_rows(coef_ref, 0, side, side, cols_total, pos_ref[1])):
        polys[index : index + 1, :] = line
    zeros = jnp.zeros((deep, HALO), ends.dtype)
    for end in (0, 1):
        near_rows = ends[end]
        window = jnp.concatenate([above, near_rows] if end == 0 else [near_rows, below], axis=0)
        window = jnp.concatenate([zeros, window, jnp.zeros((deep, LANES - HALO), ends.dtype)], axis=1)
        parts = [[] for _ in range(BASES)]
        for j in range(1, side // LANES - 1):
            summed = jnp.dot(
                window[:, j * LANES : (j + 2) * LANES], across_ref[...], preferred_element_type=jnp.float32
            )
            for b in range(BASES):
                parts[b].append(summed[:, b * LANES : (b + 1) * LANES].astype(ends.dtype))
        smoothed = [
            jnp.dot(
                down_ref[b, :HALO, :deep], jnp.concatenate(parts[b], axis=1), preferred_element_type=jnp.float32
            )
            for b in range(BASES)
        ]
        lines[end] = minus_weighted(
            smoothed, polys, slice(LANES, LANES + inner), 0 if end == 0 else side - HALO, side, rows_total, pos_ref[0]
        )
        store = pltpu.make_async_copy(
            lines.at[end],
            out_ref.at[pl.ds((side - HALO) * end, HALO), pl.ds(LANES, inner)],
            sems.at[2 + end],
        )
        store.start()
        stores.append(store)
    for store in stores:
        store.wait()


def frame(extent, base, sent, coefficients, position, template, near, far, core, other):
    side = template.shape[0]
    taps = gauss_taps()
    return pl.pallas_call(
        functools.partial(frame_kernel, extent),
        out_shape=(
            jax.ShapeDtypeStruct((side, side), jnp.float32),
            jax.ShapeDtypeStruct((HALO, LANES), jnp.int32),
            jax.ShapeDtypeStruct((8, LANES), jnp.float32),
        ),
        in_specs=[SMEM, SMEM, VMEM, VMEM, ANY, ANY, ANY, VMEM, VMEM, ANY, ANY],
        out_specs=(ANY, VMEM, VMEM),
        scratch_shapes=[
            pltpu.VMEM((2, side, 2 * LANES), jnp.bfloat16),
            pltpu.VMEM((2, 2 * HALO, side), jnp.bfloat16),
            pltpu.VMEM((3, rim_rows(side), LANES), jnp.bfloat16),
            pltpu.VMEM((2, side + 2 * HALO, 2 * LANES), jnp.bfloat16),
            pltpu.VMEM((BASES, side + 2 * HALO, 2 * LANES), jnp.bfloat16),
            pltpu.VMEM((16, side), jnp.float32),
            pltpu.VMEM((side, 2 * LANES), jnp.float32),
            pltpu.VMEM((2, HALO, side - 2 * LANES), jnp.float32),
            pltpu.SemaphoreType.DMA((7,)),
        ],
        input_output_aliases={10: 0},
        compiler_params=pltpu.CompilerParams(vmem_limit_bytes=58 << 20),
        cost_estimate=CHEAP,
        name="matched_frame",
    )(
        coefficients, position, near, far, core, other, sent,
        jnp.asarray(across_band(taps)), jnp.asarray(down_band(taps)), template, base,
    )


def add_kernel(plan, blocks_side, blocks_ref, share_ref, base_ref, *refs):
    count = len(plan)
    messages = refs[:count]
    out_ref, held, staged, hits, slots, seen, base_sems, piece_sems = refs[count:]
    block_side = held.shape[0] // blocks_side

    def area(block):
        row, col = split_index(block, blocks_side)
        rows = pl.ds(pl.multiple_of(row * block_side, block_side), block_side)
        cols = pl.ds(pl.multiple_of(col * block_side, block_side), block_side)
        return rows, cols

    for block in range(blocks_side * blocks_side):
        seen[block] = 0

    found = jnp.int32(0)
    ends = []
    for message, (source, first) in zip(messages, plan):
        for slot in range(CAP):
            block = blocks_ref[source, first + slot]
            hits[found] = block
            slots[found] = slot
            found = found + jnp.where(block >= 0, 1, 0)
        ends.append(found)

    def fetch_base(block):
        rows, cols = area(block)
        return pltpu.make_async_copy(base_ref.at[rows, cols], held.at[rows, cols], base_sems.at[block])

    def store_base(block):
        rows, cols = area(block)
        return pltpu.make_async_copy(held.at[rows, cols], out_ref.at[rows, cols], base_sems.at[block])

    start = jnp.int32(0)
    for message, end in zip(messages, ends):

        def begin(index, carry, message=message):
            block = hits[index]
            piece = piece_at(message, slots[index], block_side)
            pltpu.make_async_copy(piece, staged.at[index], piece_sems.at[index]).start()

            @pl.when(seen[block] == 0)
            def _():
                fetch_base(block).start()
                seen[block] = 1

            return carry

        lax.fori_loop(start, end, begin, 0)
        start = end

    def add(index, carry):
        block = hits[index]
        rows, cols = area(block)
        pltpu.make_async_copy(staged.at[index], staged.at[index], piece_sems.at[index]).wait()

        @pl.when(seen[block] == 1)
        def _():
            fetch_base(block).wait()
            seen[block] = 2

        held[rows, cols] = held[rows, cols] + staged[index].astype(jnp.float32) * share_ref[0, block]
        return carry

    def store(index, carry):
        block = hits[index]

        @pl.when(seen[block] == 2)
        def _():
            store_base(block).start()
            seen[block] = 3

        return carry

    def finish(index, carry):
        block = hits[index]

        @pl.when(seen[block] == 3)
        def _():
            store_base(block).wait()
            seen[block] = 4

        return carry

    for step in (add, store, finish):
        lax.fori_loop(0, found, step, 0)


def add_pieces(name, base, blocks, shares, messages, blocks_side):
    side = base.shape[0]
    plan = tuple((source, first) for _, source, first in messages)
    arrays = [array for array, _, _ in messages]
    room = CAP * len({source for source, _ in plan}) + 8
    per_tile = blocks_side * blocks_side
    return pl.pallas_call(
        functools.partial(add_kernel, plan, blocks_side),
        out_shape=jax.ShapeDtypeStruct(base.shape, base.dtype),
        in_specs=[SMEM, SMEM, ANY] + [ANY] * len(arrays),
        out_specs=ANY,
        scratch_shapes=[
            pltpu.VMEM((side, side), jnp.float32),
            pltpu.VMEM((room, side // blocks_side, side // blocks_side), arrays[0].dtype),
            pltpu.SMEM((room,), jnp.int32),
            pltpu.SMEM((room,), jnp.int32),
            pltpu.SMEM((per_tile,), jnp.int32),
            pltpu.SemaphoreType.DMA((per_tile,)),
            pltpu.SemaphoreType.DMA((room,)),
        ],
        input_output_aliases={2: 0},
        compiler_params=pltpu.CompilerParams(vmem_limit_bytes=58 << 20),
        cost_estimate=CHEAP,
        name=name,
    )(blocks, shares, base, *arrays)


class Grid:
    def __init__(self, rows, cols):
        self.rows, self.cols = rows, cols

    def pairs(self, target):
        found = []
        for row in range(self.rows):
            for col in range(self.cols):
                to_row, to_col = target(row, col)
                if 0 <= to_row < self.rows and 0 <= to_col < self.cols:
                    found.append((row * self.cols + col, to_row * self.cols + to_col))
        return found

    def near(self, array):
        return lax.ppermute(array, ("py", "px"), self.pairs(lambda r, c: (r, c ^ 1)))

    def far(self, array):
        return lax.ppermute(array, ("py", "px"), self.pairs(lambda r, c: (r, c + 1 if c % 2 else c - 1)))

    def beyond(self, array):
        return lax.ppermute(array, ("py", "px"), self.pairs(lambda r, c: (r, c - 2 if c % 2 else c + 2)))

    def core(self, array):
        return lax.ppermute(array, ("py", "px"), self.pairs(lambda r, c: (r ^ 1, c)))

    def other(self, array):
        return lax.ppermute(array, ("py", "px"), self.pairs(lambda r, c: (r + 1 if r % 2 else r - 1, c)))


def on_device(pieces, owner_map, offsets, template, coefficients):
    bar = lax.optimization_barrier
    rows_total = lax.axis_size("py")
    cols_total = lax.axis_size("px")
    grid = Grid(rows_total, cols_total)
    my_row = lax.axis_index("py")
    my_col = lax.axis_index("px")
    position = jnp.stack([my_row, my_col]).astype(jnp.int32)
    count, block_side, _ = pieces.shape
    side = template.shape[0]
    blocks_side = side // block_side

    chunks, own_core, own_other, near_rim, far_rim, labels = order_pieces(
        owner_map, offsets, position, pieces, template, cols_total
    )

    near_strip = grid.near(near_rim)
    far_strip = grid.far(far_rim)
    x0 = grid.near(chunks[0])
    extent = (rows_total, cols_total)
    template, labels = bar((template, labels))
    base = interior(extent, coefficients, position, template)
    rest = chunks[1:]
    x1, x2, x3 = [grid.near(chunk) for chunk in rest]
    own_from = (grid.core(own_core), grid.other(own_other))
    x0, near_strip, far_strip, base, *own_from = bar((x0, near_strip, far_strip, base, *own_from))
    to_core, to_other = row_rims(position, template, near_strip, far_strip, labels)
    core_rows, other_rows = grid.core(to_core), grid.other(to_other)
    z0 = grid.beyond(x0)

    own, near, far = 0, 1, 2
    core, other = 3, 6

    x1, core_rows, other_rows = bar((x1, core_rows, other_rows))
    z1 = grid.beyond(x1)
    base, blocks, shares = frame(
        extent, base, to_core, coefficients, position, template, near_strip, far_strip, core_rows, other_rows
    )

    z0, base = bar((z0, base))
    vz0 = (grid.core(z0), grid.other(z0))
    x2, base = bar((x2, base))
    z2 = grid.beyond(x2)
    vx2 = grid.core(x2)
    z1, base = bar((z1, base))
    early = [(chunk, own, i * CAP) for i, chunk in enumerate(chunks)]
    early += [(own_from[0], core, count), (own_from[1], other, count + CAP)]
    early += [(x0, near, 0), (x1, near, CAP), (x2, near, 2 * CAP), (z0, far, 0)]
    base = add_pieces("add_early", base, blocks, shares, early, blocks_side)

    x3, base = bar((x3, base))
    vx3 = (grid.core(x3), grid.other(x3))
    vz1 = grid.core(z1)
    late = [(x3, near, 3 * CAP), (z1, far, CAP), (z2, far, 2 * CAP), (vx2, core + near, 2 * CAP)]
    late += [(vz0[0], core + far, 0), (vz0[1], other + far, 0), (vz1, core + far, CAP)]
    base = add_pieces("add_late", base, blocks, shares, late, blocks_side)
    last = [(vx3[0], core + near, 3 * CAP), (vx3[1], other + near, 3 * CAP)]
    return add_pieces("add_last", base, blocks, shares, last, blocks_side)


def solution(mesh):
    in_specs = (P(("py", "px"), None, None), P(("py", "px")), P(("py", "px")), P("py", "px"), P())
    out_specs = P("py", "px")
    return jax.shard_map(on_device, mesh=mesh, in_specs=in_specs, out_specs=out_specs, check_vma=False)
```

```python
import functools

import jax
import jax.numpy as jnp
import ml_dtypes
import numpy as np
from jax import lax
from jax.experimental import pallas as pl
from jax.experimental.pallas import tpu as pltpu
from jax.sharding import PartitionSpec as P

HALO = 16
CAP = 16
BASES = 3
DEGREE = 4
LANES = 128

sigma_fractions = (0.09375, 0.1875, 0.375)
term_powers = [(degree - power_v, power_v) for degree in range(5) for power_v in range(degree + 1)]


def gauss_taps():
    positions = np.arange(-HALO, HALO + 1).astype(np.float32)
    stacked = []
    for fraction in sigma_fractions:
        sigma = fraction * HALO
        values = np.exp(-positions * positions / np.float32(2.0 * sigma * sigma))
        stacked.append(values / np.sum(values))
    return np.stack(stacked).astype(ml_dtypes.bfloat16)


def across_band(taps):
    band = np.zeros((2 * LANES, BASES * LANES), taps.dtype)
    for b in range(BASES):
        for out in range(LANES):
            band[out : out + 2 * HALO + 1, b * LANES + out] = taps[b]
    return band


def down_band(taps):
    band = np.zeros((BASES, LANES, LANES + 2 * HALO), taps.dtype)
    for b in range(BASES):
        for out in range(LANES):
            band[b, out, out : out + 2 * HALO + 1] = taps[b]
    return band


SMEM = pl.BlockSpec(memory_space=pltpu.SMEM)
VMEM = pl.BlockSpec(memory_space=pltpu.VMEM)
ANY = pl.BlockSpec(memory_space=pl.ANY)
CHEAP = pl.CostEstimate(flops=0, bytes_accessed=0, transcendentals=0)


def split_index(index, size):
    if size & (size - 1) == 0:
        return jnp.right_shift(index, size.bit_length() - 1), jnp.bitwise_and(index, size - 1)
    return lax.div(index, size), lax.rem(index, size)


def piece_at(message, slot, block_side):
    if len(message.shape) == 3:
        return message.at[slot]
    start = slot * block_side
    if not isinstance(slot, int):
        start = pl.multiple_of(start, block_side)
    return message.at[pl.ds(start, block_side), :]


def order_kernel(cols_total, owner_ref, offset_ref, pos_ref, pieces_ref, template_ref, *refs):
    outs = refs[:-9]
    near_ref, far_ref, label_ref, held, edges, meta, order_v, order_s, sems = refs[-9:]
    count = held.shape[0]
    fetch = pltpu.make_async_copy(pieces_ref, held, sems.at[len(outs)])
    fetch.start()
    side = edges.shape[1]
    rims = [
        pltpu.make_async_copy(template_ref.at[:, :LANES], edges.at[0], sems.at[len(outs) + 2]),
        pltpu.make_async_copy(template_ref.at[:, side - LANES :], edges.at[1], sems.at[len(outs) + 3]),
    ]
    for rim in rims:
        rim.start()
    my_row, my_col = pos_ref[0], pos_ref[1]
    even_col = jnp.bitwise_and(my_col, 1) == 0
    near = 1 - 2 * jnp.bitwise_and(my_col, 1)
    core = 1 - 2 * jnp.bitwise_and(my_row, 1)

    meta[...] = jnp.zeros_like(meta)
    meta[0:1, :count] = owner_ref[...]
    meta[1:2, :count] = offset_ref[...]
    lane = lax.broadcasted_iota(jnp.int32, (1, LANES), 1)
    row, col = split_index(meta[0:1, :], cols_total)
    dy, dx = row - my_row, col - my_col
    flat = dy == 0
    to_core = dy == core
    kind = jnp.where(
        dx == 0,
        jnp.where(flat, 4, jnp.where(to_core, 5, 6)),
        jnp.where(
            dx == near,
            jnp.where(flat, 3, jnp.where(to_core, 8, 7)),
            jnp.where(flat, 2, jnp.where(to_core, 1, 0)),
        ),
    )
    kind = jnp.where(lane < count, kind, 9)
    packed = (3 * (dy + 1) + dx + 2) * 256 + meta[1:2, :]

    def both(line):
        across = jnp.broadcast_to(line.astype(jnp.float32), (LANES, LANES))
        return across, across.T

    kind_l, kind_s = both(kind)
    _, packed_s = both(packed)
    sub = lax.broadcasted_iota(jnp.int32, (LANES, LANES), 0)
    lan = lax.broadcasted_iota(jnp.int32, (LANES, LANES), 1)

    def total(flags):
        return jnp.sum(jnp.where(flags, 1.0, 0.0), axis=1, keepdims=True)

    rank = total((kind_l == kind_s) & (lan < sub))
    mine = kind_s[:, 0:1]
    before = total((kind_l < kind_s) & ((kind_l >= 7.0) | (kind_s < 7.0)))
    slot = jnp.where(mine < 7.0, before + rank, jnp.where(mine < 9.0, (count - 1.0) - before - rank, -1.0))
    extra = jnp.where(
        mine == 5.0, count + rank, jnp.where(mine == 6.0, (count + CAP) + rank, -1.0)
    )
    place = lan.astype(jnp.float32)
    here = (place == slot) | (place == extra)
    order = jnp.sum(jnp.where(here, sub.astype(jnp.float32), 0.0), axis=0, keepdims=True)
    labels = jnp.sum(jnp.where(here, packed_s, 0.0), axis=0, keepdims=True)
    order_v[...] = jnp.broadcast_to(order, order_v.shape).astype(jnp.int32)
    to_smem = pltpu.make_async_copy(order_v, order_s, sems.at[len(outs) + 1])
    to_smem.start()
    labels = labels.astype(jnp.int32)
    which = lax.broadcasted_iota(jnp.int32, label_ref.shape, 0)
    label_rows = jnp.where(
        which == 0, jnp.right_shift(labels, 8), jnp.where(which == 1, jnp.bitwise_and(labels, 255), 0)
    ).astype(jnp.float32).astype(jnp.bfloat16)
    label_ref[...] = label_rows
    near_ref[:, side:] = label_rows
    far_ref[:, side:] = label_rows
    to_smem.wait()
    fetch.wait()
    for index, out_ref in enumerate(outs):
        for slot_at in range(CAP):
            pltpu.make_async_copy(
                held.at[order_s[0, index * CAP + slot_at]], piece_at(out_ref, slot_at, held.shape[1]), sems.at[index]
            ).start()
    for rim in rims:
        rim.wait()
    for block in range(side // LANES):
        rows = slice(block * LANES, (block + 1) * LANES)
        left = edges[0, rows, :].astype(jnp.float32).T[:HALO]
        right = edges[1, rows, :].astype(jnp.float32).T[LANES - HALO :]
        near_ref[:, rows] = jnp.where(even_col, right, left).astype(near_ref.dtype)
        far_ref[:, rows] = jnp.where(even_col, left, right).astype(far_ref.dtype)
    for index, out_ref in enumerate(outs):
        pltpu.make_async_copy(outs[0], outs[0], sems.at[index]).wait()


def order_pieces(owner_map, offsets, position, pieces, template, cols_total):
    count, block_side, _ = pieces.shape
    side = template.shape[0]
    parts = count // CAP + 2
    chunk = jax.ShapeDtypeStruct((CAP, block_side, block_side), pieces.dtype)
    mail = jax.ShapeDtypeStruct((2 * CAP, block_side, block_side), pieces.dtype)
    rim = jax.ShapeDtypeStruct((HALO, side + LANES), template.dtype)
    *outs, near, far, labels = pl.pallas_call(
        functools.partial(order_kernel, cols_total),
        out_shape=(chunk,) * (parts - 2)
        + (mail, mail)
        + (rim, rim, jax.ShapeDtypeStruct((HALO, LANES), template.dtype)),
        in_specs=[VMEM, VMEM, SMEM, ANY, ANY],
        out_specs=(ANY,) * parts + (VMEM,) * 3,
        scratch_shapes=[
            pltpu.VMEM(pieces.shape, pieces.dtype),
            pltpu.VMEM((2, side, LANES), template.dtype),
            pltpu.VMEM((8, LANES), jnp.int32),
            pltpu.VMEM((8, LANES), jnp.int32),
            pltpu.SMEM((8, LANES), jnp.int32),
            pltpu.SemaphoreType.DMA((parts + 4,)),
        ],
        compiler_params=pltpu.CompilerParams(vmem_limit_bytes=58 << 20),
        cost_estimate=CHEAP,
        name="order_pieces",
    )(owner_map.reshape(1, -1), offsets.reshape(1, -1), position, pieces, template)
    return outs[:-2], outs[-2], outs[-1], near, far, labels


def rim_rows(side):
    return HALO * (side // LANES + 3)


def row_rims_kernel(
    pos_ref, template_ref, near_ref, far_ref, label_ref, core_out, other_out, edges, packed, sems
):
    side = edges.shape[2]
    tiles = side // LANES
    fetches = [
        pltpu.make_async_copy(template_ref.at[:HALO, :], edges.at[0], sems.at[0]),
        pltpu.make_async_copy(template_ref.at[side - HALO :, :], edges.at[1], sems.at[1]),
    ]
    for fetch in fetches:
        fetch.start()
    even_row = jnp.bitwise_and(pos_ref[0], 1) == 0
    sub = lax.broadcasted_iota(jnp.int32, (HALO, LANES), 0)
    own = label_ref[...].astype(jnp.float32)
    near = near_ref[:, side:].astype(jnp.float32)
    far = far_ref[:, side:].astype(jnp.float32)
    pairs = own
    for index, table in ((1, near), (2, far)):
        for row in (0, 1):
            pairs = jnp.where(sub == 2 * index + row, table[row : row + 1, :], pairs)
    pairs = pairs.astype(label_ref.dtype)
    corners = []
    for strip in (near_ref, far_ref):
        low = strip[:, side - LANES : side].astype(jnp.float32)
        low = jnp.concatenate([low[:, LANES - HALO :], low[:, : LANES - HALO]], axis=1).astype(strip.dtype)
        corners.append((strip[:, :LANES], low))
    for fetch in fetches:
        fetch.wait()
    stores = []
    for index, (out_ref, upper) in enumerate(((core_out, jnp.logical_not(even_row)), (other_out, even_row))):
        for tile in range(tiles):
            cols = slice(tile * LANES, (tile + 1) * LANES)
            packed[index, tile * HALO : (tile + 1) * HALO, :] = jnp.where(upper, edges[0, :, cols], edges[1, :, cols])
        for corner, (top, low) in enumerate(corners):
            start = (tiles + corner) * HALO
            packed[index, start : start + HALO, :] = jnp.where(upper, top, low)
        packed[index, (tiles + 2) * HALO :, :] = pairs
        rows = out_ref.shape[0]
        stores.append(
            pltpu.make_async_copy(
                packed.at[index], out_ref.at[rows - packed.shape[1] : rows, :], sems.at[2 + index]
            )
        )
        stores[-1].start()
    for store in stores:
        store.wait()


def row_rims(position, template, near, far, labels):
    side = template.shape[0]
    message = jax.ShapeDtypeStruct((rim_rows(side), LANES), template.dtype)
    return pl.pallas_call(
        row_rims_kernel,
        out_shape=(message, message),
        in_specs=[SMEM, ANY, VMEM, VMEM, VMEM],
        out_specs=(ANY, ANY),
        scratch_shapes=[
            pltpu.VMEM((2, HALO, side), template.dtype),
            pltpu.VMEM((2, rim_rows(side), LANES), template.dtype),
            pltpu.SemaphoreType.DMA((4,)),
        ],
        compiler_params=pltpu.CompilerParams(vmem_limit_bytes=6 << 20),
        cost_estimate=CHEAP,
        name="row_rims",
    )(position, template, near, far, labels)


def forward_kernel(part_ref, core_in, other_in, core_out, other_out, sems):
    count = part_ref.shape[0]
    stores = [
        pltpu.make_async_copy(part_ref, out_ref.at[pl.ds(count, count)], sems.at[index])
        for index, out_ref in enumerate((core_out, other_out))
    ]
    for store in stores:
        store.start()
    for store in stores:
        store.wait()


def add_forwarded(part, to_core, to_other):
    message = jax.ShapeDtypeStruct(to_core.shape, to_core.dtype)
    return pl.pallas_call(
        forward_kernel,
        out_shape=(message, message),
        in_specs=[VMEM, ANY, ANY],
        out_specs=(ANY, ANY),
        scratch_shapes=[pltpu.SemaphoreType.DMA((2,))],
        input_output_aliases={1: 0, 2: 1},
        compiler_params=pltpu.CompilerParams(vmem_limit_bytes=6 << 20),
        cost_estimate=CHEAP,
        name="forward_pieces",
    )(part, to_core, to_other)


def fill_tables(even_row, even_col, own_ref, core_ref, other_ref, blocks_ref, share_ref):
    near_step = jnp.where(even_col, 1, -1)
    core_step = jnp.where(even_row, 1, -1)
    sub = lax.broadcasted_iota(jnp.int32, (LANES, LANES), 0)
    lane = lax.broadcasted_iota(jnp.int32, (LANES, LANES), 1)
    table = jnp.full((LANES, LANES), -1.0, jnp.float32)
    for group, (ref, row_step) in enumerate(((own_ref, 0), (core_ref, core_step), (other_ref, -core_step))):
        rows = ref[ref.shape[0] - HALO :, :].astype(jnp.float32)
        for index, col_step in enumerate((0, near_step, -near_step)):
            wanted = (5 - 3 * row_step - col_step) * jnp.int32(1)
            match = rows[2 * index : 2 * index + 1, :] == wanted.astype(jnp.float32)
            line = jnp.where(match, rows[2 * index + 1 : 2 * index + 2, :], -1.0)
            table = jnp.where(sub == 3 * group + index, line, table)
    blocks_ref[...] = table[: blocks_ref.shape[0]].astype(jnp.int32)
    upright = table.T
    counts = jnp.zeros((1, LANES), jnp.float32)
    for source in range(9):
        column = upright[: LANES // 2, source : source + 1]
        counts = counts + jnp.sum(
            jnp.where(column == lane[: LANES // 2].astype(jnp.float32), 1.0, 0.0), axis=0, keepdims=True
        )
    share_ref[...] = jnp.broadcast_to(1.0 / jnp.maximum(counts, 1.0), share_ref.shape)


def weight_rows(coef_ref, start, width, side, cols_total, my_col):
    col = lax.broadcasted_iota(jnp.int32, (1, width), 1) + (start + my_col * side)
    u = (col.astype(jnp.float32) + 0.5) * (2.0 / (side * cols_total)) - 1.0
    powers = [jnp.ones_like(u)]
    for _ in range(DEGREE):
        powers.append(powers[-1] * u)
    rows = []
    for b in range(BASES):
        for j in range(DEGREE + 1):
            total = jnp.zeros_like(u)
            for i in range(DEGREE + 1 - j):
                total = total + coef_ref[b, term_powers.index((i, j))] * powers[i]
            rows.append(total)
    return rows


def minus_weighted(smoothed, polys, cols, start, side, rows_total, my_row):
    shape = smoothed[0].shape
    row = lax.broadcasted_iota(jnp.int32, shape, 0) + (start + my_row * side)
    v = (row.astype(jnp.float32) + 0.5) * (2.0 / (side * rows_total)) - 1.0
    total = jnp.zeros(shape, jnp.float32)
    for b in range(BASES):
        power = b * (DEGREE + 1)
        weight = polys[power + DEGREE : power + DEGREE + 1, cols] * v
        for j in range(DEGREE - 1, 0, -1):
            weight = (weight + polys[power + j : power + j + 1, cols]) * v
        weight = weight + polys[power : power + 1, cols]
        total = total - weight * smoothed[b]
    return total


def interior_kernel(
    extent, coef_ref, pos_ref, centre_ref, across_ref, down_ref, out_ref, sides_ref, ends_ref,
    padded, across, polys, ready, sems,
):
    side = centre_ref.shape[0]
    rows_total, cols_total = extent
    inner = side - 2 * LANES
    copies = [
        pltpu.make_async_copy(centre_ref.at[:, : 2 * LANES], sides_ref.at[0], sems.at[2]),
        pltpu.make_async_copy(centre_ref.at[:, side - 2 * LANES :], sides_ref.at[1], sems.at[3]),
        pltpu.make_async_copy(centre_ref.at[: 2 * HALO, :], ends_ref.at[0], sems.at[4]),
        pltpu.make_async_copy(centre_ref.at[side - 2 * HALO :, :], ends_ref.at[1], sems.at[5]),
    ]
    for copy in copies:
        copy.start()
    reach = inner + LANES
    padded[:, :reach] = centre_ref[:, LANES - HALO : LANES - HALO + reach]
    for index, line in enumerate(weight_rows(coef_ref, LANES, inner, side, cols_total, pos_ref[1])):
        polys[index : index + 1, :] = line
    for b in range(BASES):
        across[b, :HALO, :] = jnp.zeros((HALO, inner), across.dtype)
        across[b, HALO + side :, :] = jnp.zeros((HALO, inner), across.dtype)

    tall = side // 2
    for start in (0, tall):
        for j in range(inner // LANES):
            window = padded[start : start + tall, j * LANES : (j + 2) * LANES]
            summed = jnp.dot(window, across_ref[...], preferred_element_type=jnp.float32)
            for b in range(BASES):
                across[b, HALO + start : HALO + start + tall, j * LANES : (j + 1) * LANES] = summed[
                    :, b * LANES : (b + 1) * LANES
                ].astype(across.dtype)

    wide = 256

    def send(start, slot):
        return pltpu.make_async_copy(
            ready.at[slot], out_ref.at[pl.ds(start, LANES), LANES : LANES + inner], sems.at[slot]
        )

    def down_step(step, carry):
        start = pl.multiple_of(step * LANES, LANES)
        slot = jnp.bitwise_and(step, 1)

        @pl.when(step >= 2)
        def _():
            send(start, slot).wait()

        for n in range(inner // wide):
            cols = slice(n * wide, (n + 1) * wide)
            smoothed = [
                jnp.dot(
                    down_ref[b], across[b, pl.ds(start, LANES + 2 * HALO), cols], preferred_element_type=jnp.float32
                )
                for b in range(BASES)
            ]
            ready[slot, :, cols] = minus_weighted(smoothed, polys, cols, start, side, rows_total, pos_ref[0])
        send(start, slot).start()
        return carry

    lax.fori_loop(0, side // LANES, down_step, 0)
    for slot in (0, 1):
        send(0, slot).wait()
    for copy in copies:
        copy.wait()


def interior(extent, coefficients, position, centre):
    side = centre.shape[0]
    inner = side - 2 * LANES
    taps = gauss_taps()
    return pl.pallas_call(
        functools.partial(interior_kernel, extent),
        out_shape=(
            jax.ShapeDtypeStruct((side, side), jnp.float32),
            jax.ShapeDtypeStruct((2, side, 2 * LANES), centre.dtype),
            jax.ShapeDtypeStruct((2, 2 * HALO, side), centre.dtype),
        ),
        in_specs=[SMEM, SMEM] + [VMEM] * 3,
        out_specs=(ANY, ANY, ANY),
        scratch_shapes=[
            pltpu.VMEM((side, inner + LANES), jnp.bfloat16),
            pltpu.VMEM((BASES, side + 2 * HALO, inner), jnp.bfloat16),
            pltpu.VMEM((16, inner), jnp.float32),
            pltpu.VMEM((2, LANES, inner), jnp.float32),
            pltpu.SemaphoreType.DMA((6,)),
        ],
        compiler_params=pltpu.CompilerParams(vmem_limit_bytes=40 << 20),
        cost_estimate=pl.CostEstimate(flops=int(8e9), bytes_accessed=1, transcendentals=0),
        name="matched_inside",
    )(coefficients, position, centre, jnp.asarray(across_band(taps)), jnp.asarray(down_band(taps)))


def upright(near_block, far_block, even_col):
    near_block = near_block.astype(jnp.float32)
    far_block = far_block.astype(jnp.float32)
    empty = jnp.zeros((LANES - HALO, LANES), jnp.float32)
    left = jnp.concatenate([jnp.where(even_col, far_block, near_block), empty], axis=0).T
    right = jnp.concatenate([jnp.where(even_col, near_block, far_block), empty], axis=0).T
    return left.astype(jnp.bfloat16), right.astype(jnp.bfloat16)


def sides_kernel(
    extent, coef_ref, pos_ref, near_ref, far_ref, across_ref, down_ref, sides, base_ref, out_ref,
    padded, across, polys, columns, sems,
):
    side = sides.shape[1]
    rows_total, cols_total = extent
    even_col = jnp.bitwise_and(pos_ref[1], 1) == 0
    for start, first in ((0, 0), (side - LANES, LANES)):
        for index, line in enumerate(weight_rows(coef_ref, start, LANES, side, cols_total, pos_ref[1])):
            polys[index : index + 1, first : first + LANES] = line
    for b in range(BASES):
        across[b, :HALO, :] = jnp.zeros((HALO, 2 * LANES), across.dtype)
        across[b, HALO + side :, :] = jnp.zeros((HALO, 2 * LANES), across.dtype)
    for block in range(side // LANES):
        rows = slice(block * LANES, (block + 1) * LANES)
        left, right = upright(near_ref[:, rows], far_ref[:, rows], even_col)
        padded[0, rows, :HALO] = left[:, :HALO]
        padded[1, rows, LANES + HALO :] = right[:, : LANES - HALO]
    padded[0, :, HALO:] = sides[0, :, : 2 * LANES - HALO]
    padded[1, :, : LANES + HALO] = sides[1, :, LANES - HALO :]

    tall = side // 2
    for end in (0, 1):
        for start in (0, tall):
            summed = jnp.dot(padded[end, start : start + tall, :], across_ref[...], preferred_element_type=jnp.float32)
            for b in range(BASES):
                across[b, HALO + start : HALO + start + tall, end * LANES : (end + 1) * LANES] = summed[
                    :, b * LANES : (b + 1) * LANES
                ].astype(across.dtype)
    both = slice(0, 2 * LANES)

    def down_step(step, carry):
        start = pl.multiple_of(step * LANES, LANES)
        smoothed = [
            jnp.dot(down_ref[b], across[b, pl.ds(start, LANES + 2 * HALO), :], preferred_element_type=jnp.float32)
            for b in range(BASES)
        ]
        columns[pl.ds(start, LANES), :] = minus_weighted(smoothed, polys, both, start, side, rows_total, pos_ref[0])
        return carry

    lax.fori_loop(0, side // LANES, down_step, 0)
    stores = [
        pltpu.make_async_copy(columns.at[:, :LANES], out_ref.at[:, :LANES], sems.at[0]),
        pltpu.make_async_copy(columns.at[:, LANES:], out_ref.at[:, side - LANES :], sems.at[1]),
    ]
    for store in stores:
        store.start()
    for store in stores:
        store.wait()


def matched_sides(extent, base, coefficients, position, sides, near, far):
    side = sides.shape[1]
    taps = gauss_taps()
    return pl.pallas_call(
        functools.partial(sides_kernel, extent),
        out_shape=jax.ShapeDtypeStruct((side, side), jnp.float32),
        in_specs=[SMEM, SMEM, VMEM, VMEM, VMEM, VMEM, VMEM, ANY],
        out_specs=ANY,
        scratch_shapes=[
            pltpu.VMEM((2, side, 2 * LANES), jnp.bfloat16),
            pltpu.VMEM((BASES, side + 2 * HALO, 2 * LANES), jnp.bfloat16),
            pltpu.VMEM((16, 2 * LANES), jnp.float32),
            pltpu.VMEM((side, 2 * LANES), jnp.float32),
            pltpu.SemaphoreType.DMA((2,)),
        ],
        input_output_aliases={7: 0},
        compiler_params=pltpu.CompilerParams(vmem_limit_bytes=16 << 20),
        cost_estimate=CHEAP,
        name="matched_sides",
    )(
        coefficients, position, near, far, jnp.asarray(across_band(taps)), jnp.asarray(down_band(taps)), sides, base
    )


def ends_kernel(
    extent, coef_ref, pos_ref, near_ref, far_ref, core_ref, other_ref, sent_ref, across_ref, down_ref, ends,
    base_ref, out_ref, blocks_ref, share_ref, window, polys, lines, sems,
):
    side = ends.shape[2]
    rows_total, cols_total = extent
    deep = 3 * HALO
    tiles = side // LANES
    even_row = jnp.bitwise_and(pos_ref[0], 1) == 0
    even_col = jnp.bitwise_and(pos_ref[1], 1) == 0
    fill_tables(even_row, even_col, sent_ref, core_ref, other_ref, blocks_ref, share_ref)
    for index, line in enumerate(weight_rows(coef_ref, 0, side, side, cols_total, pos_ref[1])):
        polys[index : index + 1, :] = line
    window[...] = jnp.zeros_like(window)
    core_rim, other_rim = core_ref[...], other_ref[...]
    near_corner = slice(tiles * HALO, (tiles + 1) * HALO)
    far_corner = slice((tiles + 1) * HALO, (tiles + 2) * HALO)
    centre = slice(HALO, HALO + side)
    right_cols = slice(HALO + side, side + LANES)
    for end, upper in ((0, even_row), (1, jnp.logical_not(even_row))):
        rim = jnp.where(upper, other_rim, core_rim)
        first = end * deep
        outer = first + (2 * HALO if end else 0)
        inner = first + (0 if end else HALO)
        left, right = upright(rim[near_corner], rim[far_corner], even_col)
        window[outer : outer + HALO, :HALO] = left[:HALO, :HALO]
        window[outer : outer + HALO, right_cols] = right[:HALO, : LANES - HALO]
        window[outer : outer + HALO, centre] = jnp.concatenate(
            [rim[tile * HALO : (tile + 1) * HALO] for tile in range(tiles)], axis=1
        )
        cols = slice(side - LANES, side) if end else slice(0, LANES)
        left, right = upright(near_ref[:, cols], far_ref[:, cols], even_col)
        rows = slice(LANES - 2 * HALO, LANES) if end else slice(0, 2 * HALO)
        window[inner : inner + 2 * HALO, :HALO] = left[rows, :HALO]
        window[inner : inner + 2 * HALO, right_cols] = right[rows, : LANES - HALO]
    for end in (0, 1):
        inner = end * deep + (0 if end else HALO)
        window[inner : inner + 2 * HALO, centre] = ends[end]

    parts = [[] for _ in range(BASES)]
    for j in range(tiles):
        summed = jnp.dot(
            window[:, j * LANES : (j + 2) * LANES], across_ref[...], preferred_element_type=jnp.float32
        )
        for b in range(BASES):
            parts[b].append(summed[:, b * LANES : (b + 1) * LANES].astype(ends.dtype))
    across = [jnp.concatenate(part, axis=1) for part in parts]
    stores = []
    for end in (0, 1):
        smoothed = [
            jnp.dot(
                down_ref[b, :HALO, :deep], across[b][end * deep : (end + 1) * deep], preferred_element_type=jnp.float32
            )
            for b in range(BASES)
        ]
        start = end * (side - HALO)
        lines[end] = minus_weighted(smoothed, polys, slice(0, side), start, side, rows_total, pos_ref[0])
        stores.append(pltpu.make_async_copy(lines.at[end], out_ref.at[start : start + HALO, :], sems.at[end]))
        stores[-1].start()
    for store in stores:
        store.wait()


def matched_ends(extent, base, sent, coefficients, position, ends, near, far, core, other):
    side = ends.shape[2]
    taps = gauss_taps()
    return pl.pallas_call(
        functools.partial(ends_kernel, extent),
        out_shape=(
            jax.ShapeDtypeStruct((side, side), jnp.float32),
            jax.ShapeDtypeStruct((HALO, LANES), jnp.int32),
            jax.ShapeDtypeStruct((8, LANES), jnp.float32),
        ),
        in_specs=[SMEM, SMEM] + [VMEM] * 8 + [ANY],
        out_specs=(ANY, VMEM, VMEM),
        scratch_shapes=[
            pltpu.VMEM((6 * HALO, side + LANES), jnp.bfloat16),
            pltpu.VMEM((16, side), jnp.float32),
            pltpu.VMEM((2, HALO, side), jnp.float32),
            pltpu.SemaphoreType.DMA((2,)),
        ],
        input_output_aliases={10: 0},
        compiler_params=pltpu.CompilerParams(vmem_limit_bytes=10 << 20),
        cost_estimate=CHEAP,
        name="matched_ends",
    )(
        coefficients, position, near, far, core, other, sent,
        jnp.asarray(across_band(taps)), jnp.asarray(down_band(taps)), ends, base,
    )


def add_kernel(plan, blocks_side, whole, blocks_ref, share_ref, base_ref, *refs):
    count = len(plan)
    messages = refs[:count]
    out_ref, held, hits, slots, seen, sems = refs[count:]
    side = held.shape[0]
    block_side = side // blocks_side
    bands = [
        pl.ds(band * block_side, block_side) if whole else None for band in range(blocks_side if whole else 0)
    ]
    for index, band in enumerate(bands):
        pltpu.make_async_copy(base_ref.at[band, :], held.at[band, :], sems.at[index]).start()

    def area(block):
        row, col = split_index(block, blocks_side)
        rows = pl.ds(pl.multiple_of(row * block_side, block_side), block_side)
        cols = pl.ds(pl.multiple_of(col * block_side, block_side), block_side)
        return rows, cols

    if not whole:
        for block in range(blocks_side * blocks_side):
            seen[block] = 0

    found = jnp.int32(0)
    ends = []
    for source, first, skipped in plan:
        for slot in range(CAP):
            block = blocks_ref[source, first + slot]
            hits[found] = block
            slots[found] = skipped + slot
            found = found + jnp.where(block >= 0, 1, 0)
        ends.append(found)

    def fetch_base(block):
        rows, cols = area(block)
        return pltpu.make_async_copy(base_ref.at[rows, cols], held.at[rows, cols], sems.at[block])

    def store_base(block):
        rows, cols = area(block)
        return pltpu.make_async_copy(held.at[rows, cols], out_ref.at[rows, cols], sems.at[block])

    def once(stage, action):
        def step(index, carry):
            block = hits[index]

            @pl.when(seen[block] == stage)
            def _():
                action(block)
                seen[block] = stage + 1

            return carry

        lax.fori_loop(0, found, step, 0)

    if whole:
        for index, band in enumerate(bands):
            pltpu.make_async_copy(base_ref.at[band, :], held.at[band, :], sems.at[index]).wait()
    else:
        once(0, lambda block: fetch_base(block).start())
        once(1, lambda block: fetch_base(block).wait())

    start = jnp.int32(0)
    for message, end in zip(messages, ends):

        def add(index, carry, message=message):
            block = hits[index]
            rows, cols = area(block)
            held[rows, cols] = held[rows, cols] + message[slots[index]].astype(jnp.float32) * share_ref[0, block]
            return carry

        lax.fori_loop(start, end, add, 0)
        start = end

    if whole:
        for index, band in enumerate(bands):
            pltpu.make_async_copy(held.at[band, :], out_ref.at[band, :], sems.at[index]).start()
        for index, band in enumerate(bands):
            pltpu.make_async_copy(held.at[band, :], out_ref.at[band, :], sems.at[index]).wait()
    else:
        once(2, lambda block: store_base(block).start())
        once(3, lambda block: store_base(block).wait())


def add_pieces(name, base, blocks, shares, messages, blocks_side, cost, whole):
    side = base.shape[0]
    plan = tuple((source, first, sum(skipped)) for _, source, first, *skipped in messages)
    arrays = [message[0] for message in messages]
    room = CAP * len({source for source, _, _ in plan}) + 8
    per_tile = blocks_side * blocks_side
    return pl.pallas_call(
        functools.partial(add_kernel, plan, blocks_side, whole),
        out_shape=jax.ShapeDtypeStruct(base.shape, base.dtype),
        in_specs=[SMEM, SMEM, ANY] + [VMEM] * len(arrays),
        out_specs=ANY,
        scratch_shapes=[
            pltpu.VMEM((side, side), jnp.float32),
            pltpu.SMEM((room,), jnp.int32),
            pltpu.SMEM((room,), jnp.int32),
            pltpu.SMEM((per_tile,), jnp.int32),
            pltpu.SemaphoreType.DMA((per_tile,)),
        ],
        input_output_aliases={2: 0},
        compiler_params=pltpu.CompilerParams(vmem_limit_bytes=16 << 20),
        cost_estimate=pl.CostEstimate(flops=int(cost * 1e9), bytes_accessed=0, transcendentals=0),
        name=name,
    )(blocks, shares, base, *arrays)


class Grid:
    def __init__(self, rows, cols):
        self.rows, self.cols = rows, cols

    def pairs(self, target):
        found = []
        for row in range(self.rows):
            for col in range(self.cols):
                to_row, to_col = target(row, col)
                if 0 <= to_row < self.rows and 0 <= to_col < self.cols:
                    found.append((row * self.cols + col, to_row * self.cols + to_col))
        return found

    def near(self, array):
        return lax.ppermute(array, ("py", "px"), self.pairs(lambda r, c: (r, c ^ 1)))

    def far(self, array):
        return lax.ppermute(array, ("py", "px"), self.pairs(lambda r, c: (r, c + 1 if c % 2 else c - 1)))

    def beyond(self, array):
        return lax.ppermute(array, ("py", "px"), self.pairs(lambda r, c: (r, c - 2 if c % 2 else c + 2)))

    def core(self, array):
        return lax.ppermute(array, ("py", "px"), self.pairs(lambda r, c: (r ^ 1, c)))

    def other(self, array):
        return lax.ppermute(array, ("py", "px"), self.pairs(lambda r, c: (r + 1 if r % 2 else r - 1, c)))


def on_device(pieces, owner_map, offsets, template, coefficients):
    bar = lax.optimization_barrier
    rows_total = lax.axis_size("py")
    cols_total = lax.axis_size("px")
    grid = Grid(rows_total, cols_total)
    my_row = lax.axis_index("py")
    my_col = lax.axis_index("px")
    position = jnp.stack([my_row, my_col]).astype(jnp.int32)
    count, block_side, _ = pieces.shape
    side = template.shape[0]
    blocks_side = side // block_side

    chunks, own_core, own_other, near_rim, far_rim, labels = order_pieces(
        owner_map, offsets, position, pieces, template, cols_total
    )

    near_strip = grid.near(near_rim)
    far_strip = grid.far(far_rim)
    x0, x1, x2, x3 = [grid.near(chunk) for chunk in chunks]
    extent = (rows_total, cols_total)
    template, labels = bar((template, labels))
    base, sides, ends = interior(extent, coefficients, position, template)
    x0, near_strip, far_strip, base = bar((x0, near_strip, far_strip, base))
    z0 = grid.beyond(x0)
    to_core, to_other = row_rims(position, template, near_strip, far_strip, labels)
    core_rows, other_rows = grid.core(to_core), grid.other(to_other)
    base, to_core = bar((base, to_core))
    base = matched_sides(extent, base, coefficients, position, sides, near_strip, far_strip)

    own, near, far = 0, 1, 2
    core, other = 3, 6

    x1, core_rows, other_rows, base = bar((x1, core_rows, other_rows, base))
    z1 = grid.beyond(x1)
    z0, base = bar((z0, base))
    own_core, own_other = add_forwarded(z0, own_core, own_other)
    from_core, from_other = grid.core(own_core), grid.other(own_other)
    x2, base = bar((x2, base))
    z2 = grid.beyond(x2)
    base, blocks, shares = matched_ends(
        extent, base, to_core, coefficients, position, ends, near_strip, far_strip, core_rows, other_rows
    )

    z1, base = bar((z1, base))
    early = [(chunk, own, i * CAP) for i, chunk in enumerate(chunks)]
    early += [(x0, near, 0), (x1, near, CAP), (x2, near, 2 * CAP), (z0, far, 0), (z1, far, CAP)]
    base = add_pieces("add_early", base, blocks, shares, early, blocks_side, 0, False)

    x3, base = bar((x3, base))
    vx3 = (grid.core(jnp.concatenate([z1, x2, x3], axis=0)), grid.other(x3))
    late = [(x3, near, 3 * CAP), (z2, far, 2 * CAP)]
    late += [(from_core, core, count), (from_other, other, count + CAP)]
    late += [(from_core, core + far, 0, CAP), (from_other, other + far, 0, CAP)]
    base = add_pieces("add_late", base, blocks, shares, late, blocks_side, 12, False)
    last = [(vx3[0], core + far, CAP), (vx3[0], core + near, 2 * CAP, CAP)]
    last += [(vx3[0], core + near, 3 * CAP, 2 * CAP), (vx3[1], other + near, 3 * CAP)]
    return add_pieces("add_last", base, blocks, shares, last, blocks_side, 12, False)


def solution(mesh):
    in_specs = (P(("py", "px"), None, None), P(("py", "px")), P(("py", "px")), P("py", "px"), P())
    out_specs = P("py", "px")
    return jax.shard_map(on_device, mesh=mesh, in_specs=in_specs, out_specs=out_specs, check_vma=False)
```

```python
import functools

import jax
import jax.numpy as jnp
import ml_dtypes
import numpy as np
from jax import lax
from jax.experimental import pallas as pl
from jax.experimental.pallas import tpu as pltpu
from jax.sharding import PartitionSpec as P

HALO = 16
CAP = 16
BASES = 3
DEGREE = 4
LANES = 128

sigma_fractions = (0.09375, 0.1875, 0.375)
term_powers = [(degree - power_v, power_v) for degree in range(5) for power_v in range(degree + 1)]


def gauss_taps():
    positions = np.arange(-HALO, HALO + 1).astype(np.float32)
    stacked = []
    for fraction in sigma_fractions:
        sigma = fraction * HALO
        values = np.exp(-positions * positions / np.float32(2.0 * sigma * sigma))
        stacked.append(values / np.sum(values))
    return np.stack(stacked).astype(ml_dtypes.bfloat16)


def across_band(taps):
    band = np.zeros((2 * LANES, BASES * LANES), taps.dtype)
    for b in range(BASES):
        for out in range(LANES):
            band[out : out + 2 * HALO + 1, b * LANES + out] = taps[b]
    return band


def down_band(taps):
    band = np.zeros((BASES, LANES, LANES + 2 * HALO), taps.dtype)
    for b in range(BASES):
        for out in range(LANES):
            band[b, out, out : out + 2 * HALO + 1] = taps[b]
    return band


SMEM = pl.BlockSpec(memory_space=pltpu.SMEM)
VMEM = pl.BlockSpec(memory_space=pltpu.VMEM)
ANY = pl.BlockSpec(memory_space=pl.ANY)
CHEAP = pl.CostEstimate(flops=0, bytes_accessed=0, transcendentals=0)


def split_index(index, size):
    if size & (size - 1) == 0:
        return jnp.right_shift(index, size.bit_length() - 1), jnp.bitwise_and(index, size - 1)
    return lax.div(index, size), lax.rem(index, size)


def piece_at(message, slot, block_side):
    if len(message.shape) == 3:
        return message.at[slot]
    start = slot * block_side
    if not isinstance(slot, int):
        start = pl.multiple_of(start, block_side)
    return message.at[pl.ds(start, block_side), :]


def order_kernel(cols_total, owner_ref, offset_ref, pieces_ref, template_ref, *refs):
    outs = refs[:-9]
    near_ref, far_ref, label_ref, held, edges, meta, order_v, order_s, sems = refs[-9:]
    count = held.shape[0]
    fetch = pltpu.make_async_copy(pieces_ref, held, sems.at[len(outs)])
    fetch.start()
    side = edges.shape[1]
    rims = [
        pltpu.make_async_copy(template_ref.at[:, :LANES], edges.at[0], sems.at[len(outs) + 2]),
        pltpu.make_async_copy(template_ref.at[:, side - LANES :], edges.at[1], sems.at[len(outs) + 3]),
    ]
    for rim in rims:
        rim.start()
    my_row, my_col = lax.axis_index("py"), lax.axis_index("px")
    even_col = jnp.bitwise_and(my_col, 1) == 0
    near = 1 - 2 * jnp.bitwise_and(my_col, 1)
    core = 1 - 2 * jnp.bitwise_and(my_row, 1)

    meta[...] = jnp.zeros_like(meta)
    meta[0:1, :count] = owner_ref[...]
    meta[1:2, :count] = offset_ref[...]
    lane = lax.broadcasted_iota(jnp.int32, (1, LANES), 1)
    row, col = split_index(meta[0:1, :], cols_total)
    dy, dx = row - my_row, col - my_col
    flat = dy == 0
    to_core = dy == core
    kind = jnp.where(
        dx == 0,
        jnp.where(flat, 4, jnp.where(to_core, 5, 6)),
        jnp.where(
            dx == near,
            jnp.where(flat, 3, jnp.where(to_core, 8, 7)),
            jnp.where(flat, 2, jnp.where(to_core, 1, 0)),
        ),
    )
    kind = jnp.where(lane < count, kind, 9)
    packed = (3 * (dy + 1) + dx + 2) * 256 + meta[1:2, :]

    def both(line):
        across = jnp.broadcast_to(line.astype(jnp.float32), (LANES, LANES))
        return across, across.T

    kind_l, kind_s = both(kind)
    _, packed_s = both(packed)
    sub = lax.broadcasted_iota(jnp.int32, (LANES, LANES), 0)
    lan = lax.broadcasted_iota(jnp.int32, (LANES, LANES), 1)

    def total(flags):
        return jnp.sum(jnp.where(flags, 1.0, 0.0), axis=1, keepdims=True)

    rank = total((kind_l == kind_s) & (lan < sub))
    mine = kind_s[:, 0:1]
    before = total((kind_l < kind_s) & ((kind_l >= 7.0) | (kind_s < 7.0)))
    slot = jnp.where(mine < 7.0, before + rank, jnp.where(mine < 9.0, (count - 1.0) - before - rank, -1.0))
    extra = jnp.where(
        mine == 5.0, count + rank, jnp.where(mine == 6.0, (count + CAP) + rank, -1.0)
    )
    place = lan.astype(jnp.float32)
    here = (place == slot) | (place == extra)
    order = jnp.sum(jnp.where(here, sub.astype(jnp.float32), 0.0), axis=0, keepdims=True)
    labels = jnp.sum(jnp.where(here, packed_s, 0.0), axis=0, keepdims=True)
    order_v[...] = jnp.broadcast_to(order, order_v.shape).astype(jnp.int32)
    to_smem = pltpu.make_async_copy(order_v, order_s, sems.at[len(outs) + 1])
    to_smem.start()
    labels = labels.astype(jnp.int32)
    which = lax.broadcasted_iota(jnp.int32, label_ref.shape, 0)
    label_rows = jnp.where(
        which == 0, jnp.right_shift(labels, 8), jnp.where(which == 1, jnp.bitwise_and(labels, 255), 0)
    ).astype(jnp.float32).astype(jnp.bfloat16)
    label_ref[...] = label_rows
    near_ref[:, side:] = label_rows
    far_ref[:, side:] = label_rows
    to_smem.wait()
    fetch.wait()
    for index, out_ref in enumerate(outs):
        for slot_at in range(CAP):
            pltpu.make_async_copy(
                held.at[order_s[0, index * CAP + slot_at]], piece_at(out_ref, slot_at, held.shape[1]), sems.at[index]
            ).start()
    for rim in rims:
        rim.wait()
    for block in range(side // LANES):
        rows = slice(block * LANES, (block + 1) * LANES)
        left = edges[0, rows, :].astype(jnp.float32).T[:HALO]
        right = edges[1, rows, :].astype(jnp.float32).T[LANES - HALO :]
        near_ref[:, rows] = jnp.where(even_col, right, left).astype(near_ref.dtype)
        far_ref[:, rows] = jnp.where(even_col, left, right).astype(far_ref.dtype)
    for index, out_ref in enumerate(outs):
        pltpu.make_async_copy(outs[0], outs[0], sems.at[index]).wait()


def order_pieces(owner_map, offsets, pieces, template, cols_total):
    count, block_side, _ = pieces.shape
    side = template.shape[0]
    parts = count // CAP + 2
    chunk = jax.ShapeDtypeStruct((CAP, block_side, block_side), pieces.dtype)
    mail = jax.ShapeDtypeStruct((2 * CAP, block_side, block_side), pieces.dtype)
    rim = jax.ShapeDtypeStruct((HALO, side + LANES), template.dtype)
    *outs, near, far, labels = pl.pallas_call(
        functools.partial(order_kernel, cols_total),
        out_shape=(chunk,) * (parts - 2)
        + (mail, mail)
        + (rim, rim, jax.ShapeDtypeStruct((HALO, LANES), template.dtype)),
        in_specs=[VMEM, VMEM, ANY, ANY],
        out_specs=(ANY,) * parts + (VMEM,) * 3,
        scratch_shapes=[
            pltpu.VMEM(pieces.shape, pieces.dtype),
            pltpu.VMEM((2, side, LANES), template.dtype),
            pltpu.VMEM((8, LANES), jnp.int32),
            pltpu.VMEM((8, LANES), jnp.int32),
            pltpu.SMEM((8, LANES), jnp.int32),
            pltpu.SemaphoreType.DMA((parts + 4,)),
        ],
        compiler_params=pltpu.CompilerParams(vmem_limit_bytes=58 << 20),
        cost_estimate=CHEAP,
        name="order_pieces",
    )(owner_map.reshape(1, -1), offsets.reshape(1, -1), pieces, template)
    return outs[:-2], outs[-2], outs[-1], near, far, labels


def rim_rows(side):
    return HALO * (side // LANES + 3)


def row_rims_kernel(
    template_ref, near_ref, far_ref, label_ref, core_out, other_out, edges, packed, sems
):
    side = edges.shape[2]
    tiles = side // LANES
    fetches = [
        pltpu.make_async_copy(template_ref.at[:HALO, :], edges.at[0], sems.at[0]),
        pltpu.make_async_copy(template_ref.at[side - HALO :, :], edges.at[1], sems.at[1]),
    ]
    for fetch in fetches:
        fetch.start()
    even_row = jnp.bitwise_and(lax.axis_index("py"), 1) == 0
    sub = lax.broadcasted_iota(jnp.int32, (HALO, LANES), 0)
    own = label_ref[...].astype(jnp.float32)
    near = near_ref[:, side:].astype(jnp.float32)
    far = far_ref[:, side:].astype(jnp.float32)
    pairs = own
    for index, table in ((1, near), (2, far)):
        for row in (0, 1):
            pairs = jnp.where(sub == 2 * index + row, table[row : row + 1, :], pairs)
    pairs = pairs.astype(label_ref.dtype)
    corners = []
    for strip in (near_ref, far_ref):
        low = strip[:, side - LANES : side].astype(jnp.float32)
        low = jnp.concatenate([low[:, LANES - HALO :], low[:, : LANES - HALO]], axis=1).astype(strip.dtype)
        corners.append((strip[:, :LANES], low))
    for fetch in fetches:
        fetch.wait()
    stores = []
    for index, (out_ref, upper) in enumerate(((core_out, jnp.logical_not(even_row)), (other_out, even_row))):
        for tile in range(tiles):
            cols = slice(tile * LANES, (tile + 1) * LANES)
            packed[index, tile * HALO : (tile + 1) * HALO, :] = jnp.where(upper, edges[0, :, cols], edges[1, :, cols])
        for corner, (top, low) in enumerate(corners):
            start = (tiles + corner) * HALO
            packed[index, start : start + HALO, :] = jnp.where(upper, top, low)
        packed[index, (tiles + 2) * HALO :, :] = pairs
        rows = out_ref.shape[0]
        stores.append(
            pltpu.make_async_copy(
                packed.at[index], out_ref.at[rows - packed.shape[1] : rows, :], sems.at[2 + index]
            )
        )
        stores[-1].start()
    for store in stores:
        store.wait()


def row_rims(template, near, far, labels):
    side = template.shape[0]
    message = jax.ShapeDtypeStruct((rim_rows(side), LANES), template.dtype)
    return pl.pallas_call(
        row_rims_kernel,
        out_shape=(message, message),
        in_specs=[ANY, VMEM, VMEM, VMEM],
        out_specs=(ANY, ANY),
        scratch_shapes=[
            pltpu.VMEM((2, HALO, side), template.dtype),
            pltpu.VMEM((2, rim_rows(side), LANES), template.dtype),
            pltpu.SemaphoreType.DMA((4,)),
        ],
        compiler_params=pltpu.CompilerParams(vmem_limit_bytes=6 << 20),
        cost_estimate=CHEAP,
        name="row_rims",
    )(template, near, far, labels)


def forward_kernel(part_ref, core_in, other_in, core_out, other_out, sems):
    count = part_ref.shape[0]
    stores = [
        pltpu.make_async_copy(part_ref, out_ref.at[pl.ds(count, count)], sems.at[index])
        for index, out_ref in enumerate((core_out, other_out))
    ]
    for store in stores:
        store.start()
    for store in stores:
        store.wait()


def add_forwarded(part, to_core, to_other):
    message = jax.ShapeDtypeStruct(to_core.shape, to_core.dtype)
    return pl.pallas_call(
        forward_kernel,
        out_shape=(message, message),
        in_specs=[VMEM, ANY, ANY],
        out_specs=(ANY, ANY),
        scratch_shapes=[pltpu.SemaphoreType.DMA((2,))],
        input_output_aliases={1: 0, 2: 1},
        compiler_params=pltpu.CompilerParams(vmem_limit_bytes=6 << 20),
        cost_estimate=CHEAP,
        name="forward_pieces",
    )(part, to_core, to_other)


def fill_tables(even_row, even_col, own_ref, core_ref, other_ref, blocks_ref, share_ref):
    near_step = jnp.where(even_col, 1, -1)
    core_step = jnp.where(even_row, 1, -1)
    sub = lax.broadcasted_iota(jnp.int32, (LANES, LANES), 0)
    lane = lax.broadcasted_iota(jnp.int32, (LANES, LANES), 1)
    table = jnp.full((LANES, LANES), -1.0, jnp.float32)
    for group, (ref, row_step) in enumerate(((own_ref, 0), (core_ref, core_step), (other_ref, -core_step))):
        rows = ref[ref.shape[0] - HALO :, :].astype(jnp.float32)
        for index, col_step in enumerate((0, near_step, -near_step)):
            wanted = (5 - 3 * row_step - col_step) * jnp.int32(1)
            match = rows[2 * index : 2 * index + 1, :] == wanted.astype(jnp.float32)
            line = jnp.where(match, rows[2 * index + 1 : 2 * index + 2, :], -1.0)
            table = jnp.where(sub == 3 * group + index, line, table)
    blocks_ref[...] = table[: blocks_ref.shape[0]].astype(jnp.int32)
    upright = table.T
    counts = jnp.zeros((1, LANES), jnp.float32)
    for source in range(9):
        column = upright[: LANES // 2, source : source + 1]
        counts = counts + jnp.sum(
            jnp.where(column == lane[: LANES // 2].astype(jnp.float32), 1.0, 0.0), axis=0, keepdims=True
        )
    share_ref[...] = jnp.broadcast_to(1.0 / jnp.maximum(counts, 1.0), share_ref.shape)


def weight_rows(coef_ref, start, width, side, cols_total, my_col):
    col = lax.broadcasted_iota(jnp.int32, (1, width), 1) + (start + my_col * side)
    u = (col.astype(jnp.float32) + 0.5) * (2.0 / (side * cols_total)) - 1.0
    powers = [jnp.ones_like(u)]
    for _ in range(DEGREE):
        powers.append(powers[-1] * u)
    rows = []
    for b in range(BASES):
        for j in range(DEGREE + 1):
            total = jnp.zeros_like(u)
            for i in range(DEGREE + 1 - j):
                total = total + coef_ref[b, term_powers.index((i, j))] * powers[i]
            rows.append(total)
    return rows


def minus_weighted(smoothed, polys, cols, start, side, rows_total, my_row):
    shape = smoothed[0].shape
    row = lax.broadcasted_iota(jnp.int32, shape, 0) + (start + my_row * side)
    v = (row.astype(jnp.float32) + 0.5) * (2.0 / (side * rows_total)) - 1.0
    total = jnp.zeros(shape, jnp.float32)
    for b in range(BASES):
        power = b * (DEGREE + 1)
        weight = polys[power + DEGREE : power + DEGREE + 1, cols] * v
        for j in range(DEGREE - 1, 0, -1):
            weight = (weight + polys[power + j : power + j + 1, cols]) * v
        weight = weight + polys[power : power + 1, cols]
        total = total - weight * smoothed[b]
    return total


def interior_kernel(
    extent, coef_ref, centre_ref, across_ref, down_ref, out_ref, sides_ref, ends_ref,
    padded, across, polys, ready, sems,
):
    side = centre_ref.shape[0]
    rows_total, cols_total = extent
    inner = side - 2 * LANES
    copies = [
        pltpu.make_async_copy(centre_ref.at[:, : 2 * LANES], sides_ref.at[0], sems.at[2]),
        pltpu.make_async_copy(centre_ref.at[:, side - 2 * LANES :], sides_ref.at[1], sems.at[3]),
        pltpu.make_async_copy(centre_ref.at[: 2 * HALO, :], ends_ref.at[0], sems.at[4]),
        pltpu.make_async_copy(centre_ref.at[side - 2 * HALO :, :], ends_ref.at[1], sems.at[5]),
    ]
    for copy in copies:
        copy.start()
    reach = inner + LANES
    padded[:, :reach] = centre_ref[:, LANES - HALO : LANES - HALO + reach]
    for index, line in enumerate(weight_rows(coef_ref, LANES, inner, side, cols_total, lax.axis_index("px"))):
        polys[index : index + 1, :] = line
    for b in range(BASES):
        across[b, :HALO, :] = jnp.zeros((HALO, inner), across.dtype)
        across[b, HALO + side :, :] = jnp.zeros((HALO, inner), across.dtype)

    tall = side // 2
    for start in (0, tall):
        for j in range(inner // LANES):
            window = padded[start : start + tall, j * LANES : (j + 2) * LANES]
            summed = jnp.dot(window, across_ref[...], preferred_element_type=jnp.float32)
            for b in range(BASES):
                across[b, HALO + start : HALO + start + tall, j * LANES : (j + 1) * LANES] = summed[
                    :, b * LANES : (b + 1) * LANES
                ].astype(across.dtype)

    wide = 256

    def send(start, slot):
        return pltpu.make_async_copy(
            ready.at[slot], out_ref.at[pl.ds(start, LANES), LANES : LANES + inner], sems.at[slot]
        )

    def down_step(step, carry):
        start = pl.multiple_of(step * LANES, LANES)
        slot = jnp.bitwise_and(step, 1)

        @pl.when(step >= 2)
        def _():
            send(start, slot).wait()

        for n in range(inner // wide):
            cols = slice(n * wide, (n + 1) * wide)
            smoothed = [
                jnp.dot(
                    down_ref[b], across[b, pl.ds(start, LANES + 2 * HALO), cols], preferred_element_type=jnp.float32
                )
                for b in range(BASES)
            ]
            ready[slot, :, cols] = minus_weighted(smoothed, polys, cols, start, side, rows_total, lax.axis_index("py"))
        send(start, slot).start()
        return carry

    lax.fori_loop(0, side // LANES, down_step, 0)
    for slot in (0, 1):
        send(0, slot).wait()
    for copy in copies:
        copy.wait()


def interior(extent, coefficients, centre):
    side = centre.shape[0]
    inner = side - 2 * LANES
    taps = gauss_taps()
    return pl.pallas_call(
        functools.partial(interior_kernel, extent),
        out_shape=(
            jax.ShapeDtypeStruct((side, side), jnp.float32),
            jax.ShapeDtypeStruct((2, side, 2 * LANES), centre.dtype),
            jax.ShapeDtypeStruct((2, 2 * HALO, side), centre.dtype),
        ),
        in_specs=[SMEM] + [VMEM] * 3,
        out_specs=(ANY, ANY, ANY),
        scratch_shapes=[
            pltpu.VMEM((side, inner + LANES), jnp.bfloat16),
            pltpu.VMEM((BASES, side + 2 * HALO, inner), jnp.bfloat16),
            pltpu.VMEM((16, inner), jnp.float32),
            pltpu.VMEM((2, LANES, inner), jnp.float32),
            pltpu.SemaphoreType.DMA((6,)),
        ],
        compiler_params=pltpu.CompilerParams(vmem_limit_bytes=40 << 20),
        cost_estimate=pl.CostEstimate(flops=int(8e9), bytes_accessed=1, transcendentals=0),
        name="matched_inside",
    )(coefficients, centre, jnp.asarray(across_band(taps)), jnp.asarray(down_band(taps)))


def upright(near_block, far_block, even_col):
    near_block = near_block.astype(jnp.float32)
    far_block = far_block.astype(jnp.float32)
    empty = jnp.zeros((LANES - HALO, LANES), jnp.float32)
    left = jnp.concatenate([jnp.where(even_col, far_block, near_block), empty], axis=0).T
    right = jnp.concatenate([jnp.where(even_col, near_block, far_block), empty], axis=0).T
    return left.astype(jnp.bfloat16), right.astype(jnp.bfloat16)


def sides_kernel(
    extent, coef_ref, near_ref, far_ref, across_ref, down_ref, sides, base_ref, out_ref,
    padded, across, polys, columns, sems,
):
    side = sides.shape[1]
    rows_total, cols_total = extent
    even_col = jnp.bitwise_and(lax.axis_index("px"), 1) == 0
    for start, first in ((0, 0), (side - LANES, LANES)):
        for index, line in enumerate(weight_rows(coef_ref, start, LANES, side, cols_total, lax.axis_index("px"))):
            polys[index : index + 1, first : first + LANES] = line
    for b in range(BASES):
        across[b, :HALO, :] = jnp.zeros((HALO, 2 * LANES), across.dtype)
        across[b, HALO + side :, :] = jnp.zeros((HALO, 2 * LANES), across.dtype)
    for block in range(side // LANES):
        rows = slice(block * LANES, (block + 1) * LANES)
        left, right = upright(near_ref[:, rows], far_ref[:, rows], even_col)
        padded[0, rows, :HALO] = left[:, :HALO]
        padded[1, rows, LANES + HALO :] = right[:, : LANES - HALO]
    padded[0, :, HALO:] = sides[0, :, : 2 * LANES - HALO]
    padded[1, :, : LANES + HALO] = sides[1, :, LANES - HALO :]

    tall = side // 2
    for end in (0, 1):
        for start in (0, tall):
            summed = jnp.dot(padded[end, start : start + tall, :], across_ref[...], preferred_element_type=jnp.float32)
            for b in range(BASES):
                across[b, HALO + start : HALO + start + tall, end * LANES : (end + 1) * LANES] = summed[
                    :, b * LANES : (b + 1) * LANES
                ].astype(across.dtype)
    both = slice(0, 2 * LANES)

    def send(rows, end):
        return pltpu.make_async_copy(
            columns.at[rows, pl.ds(end * LANES, LANES)],
            out_ref.at[rows, pl.ds(end * (side - LANES), LANES)],
            sems.at[end],
        )

    def down_step(step, carry):
        start = pl.multiple_of(step * LANES, LANES)
        smoothed = [
            jnp.dot(down_ref[b], across[b, pl.ds(start, LANES + 2 * HALO), :], preferred_element_type=jnp.float32)
            for b in range(BASES)
        ]
        rows = pl.ds(start, LANES)
        columns[rows, :] = minus_weighted(
            smoothed, polys, both, start, side, rows_total, lax.axis_index("py")
        )
        for end in (0, 1):
            send(rows, end).start()
        return carry

    lax.fori_loop(0, side // LANES, down_step, 0)
    for end in (0, 1):
        send(pl.ds(0, side), end).wait()


def matched_sides(extent, base, coefficients, sides, near, far):
    side = sides.shape[1]
    taps = gauss_taps()
    return pl.pallas_call(
        functools.partial(sides_kernel, extent),
        out_shape=jax.ShapeDtypeStruct((side, side), jnp.float32),
        in_specs=[SMEM, VMEM, VMEM, VMEM, VMEM, VMEM, ANY],
        out_specs=ANY,
        scratch_shapes=[
            pltpu.VMEM((2, side, 2 * LANES), jnp.bfloat16),
            pltpu.VMEM((BASES, side + 2 * HALO, 2 * LANES), jnp.bfloat16),
            pltpu.VMEM((16, 2 * LANES), jnp.float32),
            pltpu.VMEM((side, 2 * LANES), jnp.float32),
            pltpu.SemaphoreType.DMA((2,)),
        ],
        input_output_aliases={6: 0},
        compiler_params=pltpu.CompilerParams(vmem_limit_bytes=16 << 20),
        cost_estimate=CHEAP,
        name="matched_sides",
    )(
        coefficients, near, far, jnp.asarray(across_band(taps)), jnp.asarray(down_band(taps)), sides, base
    )


def ends_kernel(
    extent, coef_ref, near_ref, far_ref, core_ref, other_ref, sent_ref, across_ref, down_ref, ends,
    base_ref, out_ref, blocks_ref, share_ref, window, polys, lines, sems,
):
    side = ends.shape[2]
    rows_total, cols_total = extent
    deep = 3 * HALO
    tiles = side // LANES
    even_row = jnp.bitwise_and(lax.axis_index("py"), 1) == 0
    even_col = jnp.bitwise_and(lax.axis_index("px"), 1) == 0
    fill_tables(even_row, even_col, sent_ref, core_ref, other_ref, blocks_ref, share_ref)
    for index, line in enumerate(weight_rows(coef_ref, 0, side, side, cols_total, lax.axis_index("px"))):
        polys[index : index + 1, :] = line
    window[...] = jnp.zeros_like(window)
    core_rim, other_rim = core_ref[...], other_ref[...]
    near_corner = slice(tiles * HALO, (tiles + 1) * HALO)
    far_corner = slice((tiles + 1) * HALO, (tiles + 2) * HALO)
    centre = slice(HALO, HALO + side)
    right_cols = slice(HALO + side, side + LANES)
    for end, upper in ((0, even_row), (1, jnp.logical_not(even_row))):
        rim = jnp.where(upper, other_rim, core_rim)
        first = end * deep
        outer = first + (2 * HALO if end else 0)
        inner = first + (0 if end else HALO)
        left, right = upright(rim[near_corner], rim[far_corner], even_col)
        window[outer : outer + HALO, :HALO] = left[:HALO, :HALO]
        window[outer : outer + HALO, right_cols] = right[:HALO, : LANES - HALO]
        window[outer : outer + HALO, centre] = jnp.concatenate(
            [rim[tile * HALO : (tile + 1) * HALO] for tile in range(tiles)], axis=1
        )
        cols = slice(side - LANES, side) if end else slice(0, LANES)
        left, right = upright(near_ref[:, cols], far_ref[:, cols], even_col)
        rows = slice(LANES - 2 * HALO, LANES) if end else slice(0, 2 * HALO)
        window[inner : inner + 2 * HALO, :HALO] = left[rows, :HALO]
        window[inner : inner + 2 * HALO, right_cols] = right[rows, : LANES - HALO]
    for end in (0, 1):
        inner = end * deep + (0 if end else HALO)
        window[inner : inner + 2 * HALO, centre] = ends[end]

    parts = [[] for _ in range(BASES)]
    for j in range(tiles):
        summed = jnp.dot(
            window[:, j * LANES : (j + 2) * LANES], across_ref[...], preferred_element_type=jnp.float32
        )
        for b in range(BASES):
            parts[b].append(summed[:, b * LANES : (b + 1) * LANES].astype(ends.dtype))
    across = [jnp.concatenate(part, axis=1) for part in parts]
    stores = []
    for end in (0, 1):
        smoothed = [
            jnp.dot(
                down_ref[b, :HALO, :deep], across[b][end * deep : (end + 1) * deep], preferred_element_type=jnp.float32
            )
            for b in range(BASES)
        ]
        start = end * (side - HALO)
        lines[end] = minus_weighted(smoothed, polys, slice(0, side), start, side, rows_total, lax.axis_index("py"))
        stores.append(pltpu.make_async_copy(lines.at[end], out_ref.at[start : start + HALO, :], sems.at[end]))
        stores[-1].start()
    for store in stores:
        store.wait()


def matched_ends(extent, base, sent, coefficients, ends, near, far, core, other):
    side = ends.shape[2]
    taps = gauss_taps()
    return pl.pallas_call(
        functools.partial(ends_kernel, extent),
        out_shape=(
            jax.ShapeDtypeStruct((side, side), jnp.float32),
            jax.ShapeDtypeStruct((HALO, LANES), jnp.int32),
            jax.ShapeDtypeStruct((8, LANES), jnp.float32),
        ),
        in_specs=[SMEM] + [VMEM] * 8 + [ANY],
        out_specs=(ANY, VMEM, VMEM),
        scratch_shapes=[
            pltpu.VMEM((6 * HALO, side + LANES), jnp.bfloat16),
            pltpu.VMEM((16, side), jnp.float32),
            pltpu.VMEM((2, HALO, side), jnp.float32),
            pltpu.SemaphoreType.DMA((2,)),
        ],
        input_output_aliases={9: 0},
        compiler_params=pltpu.CompilerParams(vmem_limit_bytes=10 << 20),
        cost_estimate=CHEAP,
        name="matched_ends",
    )(
        coefficients, near, far, core, other, sent,
        jnp.asarray(across_band(taps)), jnp.asarray(down_band(taps)), ends, base,
    )


def add_kernel(plan, blocks_side, blocks_ref, share_ref, base_ref, *refs):
    count = len(plan)
    messages = refs[:count]
    out_ref, held, hits, slots, left, seen, sems = refs[count:]
    block_side = held.shape[0] // blocks_side

    def area(block):
        row, col = split_index(block, blocks_side)
        rows = pl.ds(pl.multiple_of(row * block_side, block_side), block_side)
        cols = pl.ds(pl.multiple_of(col * block_side, block_side), block_side)
        return rows, cols

    for block in range(blocks_side * blocks_side):
        left[block] = 0
        seen[block] = 0

    found = jnp.int32(0)
    ends = []
    for source, first, skipped in plan:
        for slot in range(CAP):
            block = blocks_ref[source, first + slot]
            hits[found] = block
            slots[found] = skipped + slot
            found = found + jnp.where(block >= 0, 1, 0)
        ends.append(found)

    def fetch_base(block):
        rows, cols = area(block)
        return pltpu.make_async_copy(base_ref.at[rows, cols], held.at[rows, cols], sems.at[block])

    def store_base(block):
        rows, cols = area(block)
        return pltpu.make_async_copy(held.at[rows, cols], out_ref.at[rows, cols], sems.at[block])

    def begin(index, carry):
        block = hits[index]
        left[block] = left[block] + 1

        @pl.when(seen[block] == 0)
        def _():
            fetch_base(block).start()
            seen[block] = 1

        return carry

    lax.fori_loop(0, found, begin, 0)

    start = jnp.int32(0)
    for message, end in zip(messages, ends):

        def add(index, carry, message=message):
            block = hits[index]
            rows, cols = area(block)

            @pl.when(seen[block] == 1)
            def _():
                fetch_base(block).wait()
                seen[block] = 2

            held[rows, cols] = held[rows, cols] + message[slots[index]].astype(jnp.float32) * share_ref[0, block]
            more = left[block] - 1
            left[block] = more

            @pl.when(more == 0)
            def _():
                store_base(block).start()

            return carry

        lax.fori_loop(start, end, add, 0)
        start = end

    def finish(index, carry):
        block = hits[index]

        @pl.when(seen[block] == 2)
        def _():
            store_base(block).wait()
            seen[block] = 3

        return carry

    lax.fori_loop(0, found, finish, 0)


def add_pieces(name, base, blocks, shares, messages, blocks_side, cost):
    side = base.shape[0]
    plan = tuple((source, first, sum(skipped)) for _, source, first, *skipped in messages)
    arrays = [message[0] for message in messages]
    room = CAP * len({source for source, _, _ in plan}) + 8
    per_tile = blocks_side * blocks_side
    return pl.pallas_call(
        functools.partial(add_kernel, plan, blocks_side),
        out_shape=jax.ShapeDtypeStruct(base.shape, base.dtype),
        in_specs=[SMEM, SMEM, ANY] + [VMEM] * len(arrays),
        out_specs=ANY,
        scratch_shapes=[
            pltpu.VMEM((side, side), jnp.float32),
            pltpu.SMEM((room,), jnp.int32),
            pltpu.SMEM((room,), jnp.int32),
            pltpu.SMEM((per_tile,), jnp.int32),
            pltpu.SMEM((per_tile,), jnp.int32),
            pltpu.SemaphoreType.DMA((per_tile,)),
        ],
        input_output_aliases={2: 0},
        compiler_params=pltpu.CompilerParams(vmem_limit_bytes=16 << 20),
        cost_estimate=pl.CostEstimate(flops=int(cost * 1e9), bytes_accessed=0, transcendentals=0),
        name=name,
    )(blocks, shares, base, *arrays)


class Grid:
    def __init__(self, rows, cols):
        self.rows, self.cols = rows, cols

    def pairs(self, target):
        found = []
        for row in range(self.rows):
            for col in range(self.cols):
                to_row, to_col = target(row, col)
                if 0 <= to_row < self.rows and 0 <= to_col < self.cols:
                    found.append((row * self.cols + col, to_row * self.cols + to_col))
        return found

    def near(self, array):
        return lax.ppermute(array, ("py", "px"), self.pairs(lambda r, c: (r, c ^ 1)))

    def far(self, array):
        return lax.ppermute(array, ("py", "px"), self.pairs(lambda r, c: (r, c + 1 if c % 2 else c - 1)))

    def beyond(self, array):
        return lax.ppermute(array, ("py", "px"), self.pairs(lambda r, c: (r, c - 2 if c % 2 else c + 2)))

    def core(self, array):
        return lax.ppermute(array, ("py", "px"), self.pairs(lambda r, c: (r ^ 1, c)))

    def other(self, array):
        return lax.ppermute(array, ("py", "px"), self.pairs(lambda r, c: (r + 1 if r % 2 else r - 1, c)))


def on_device(pieces, owner_map, offsets, template, coefficients):
    bar = lax.optimization_barrier
    rows_total = lax.axis_size("py")
    cols_total = lax.axis_size("px")
    grid = Grid(rows_total, cols_total)
    count, block_side, _ = pieces.shape
    side = template.shape[0]
    blocks_side = side // block_side

    chunks, own_core, own_other, near_rim, far_rim, labels = order_pieces(
        owner_map, offsets, pieces, template, cols_total
    )

    near_strip = grid.near(near_rim)
    far_strip = grid.far(far_rim)
    x0, x1, x2, x3 = [grid.near(chunk) for chunk in chunks]
    extent = (rows_total, cols_total)
    template, labels = bar((template, labels))
    base, sides, ends = interior(extent, coefficients, template)
    x0, near_strip, far_strip, base = bar((x0, near_strip, far_strip, base))
    z0 = grid.beyond(x0)
    to_core, to_other = row_rims(template, near_strip, far_strip, labels)
    other_rows, core_rows = grid.other(to_other), grid.core(to_core)
    x1, core_rows, other_rows, base = bar((x1, core_rows, other_rows, base))
    z1 = grid.beyond(x1)
    base = matched_sides(extent, base, coefficients, sides, near_strip, far_strip)

    own, near, far = 0, 1, 2
    core, other = 3, 6

    z0, base = bar((z0, base))
    own_core, own_other = add_forwarded(z0, own_core, own_other)
    from_core, from_other = grid.core(own_core), grid.other(own_other)
    x2, base = bar((x2, base))
    z2 = grid.beyond(x2)
    base, blocks, shares = matched_ends(
        extent, base, to_core, coefficients, ends, near_strip, far_strip, core_rows, other_rows
    )

    z1, base = bar((z1, base))
    early = [(chunk, own, i * CAP) for i, chunk in enumerate(chunks)]
    early += [(x0, near, 0), (x1, near, CAP), (x2, near, 2 * CAP), (z0, far, 0), (z1, far, CAP)]
    base = add_pieces("add_early", base, blocks, shares, early, blocks_side, 0)

    x3, base = bar((x3, base))
    vx3 = (grid.core(jnp.concatenate([z1, x2, x3], axis=0)), grid.other(x3))
    late = [(x3, near, 3 * CAP), (z2, far, 2 * CAP)]
    late += [(from_core, core, count), (from_other, other, count + CAP)]
    late += [(from_core, core + far, 0, CAP), (from_other, other + far, 0, CAP)]
    base = add_pieces("add_late", base, blocks, shares, late, blocks_side, 12)
    last = [(vx3[0], core + far, CAP), (vx3[0], core + near, 2 * CAP, CAP)]
    last += [(vx3[0], core + near, 3 * CAP, 2 * CAP), (vx3[1], other + near, 3 * CAP)]
    return add_pieces("add_last", base, blocks, shares, last, blocks_side, 12)


def solution(mesh):
    in_specs = (P(("py", "px"), None, None), P(("py", "px")), P(("py", "px")), P("py", "px"), P())
    out_specs = P("py", "px")
    return jax.shard_map(on_device, mesh=mesh, in_specs=in_specs, out_specs=out_specs, check_vma=False)
```

```python
import functools

import jax
import jax.numpy as jnp
import ml_dtypes
import numpy as np
from jax import lax
from jax.experimental import pallas as pl
from jax.experimental.pallas import tpu as pltpu
from jax.sharding import PartitionSpec as P

HALO = 16
CAP = 16
BASES = 3
DEGREE = 4
LANES = 128

sigma_fractions = (0.09375, 0.1875, 0.375)
term_powers = [(degree - power_v, power_v) for degree in range(5) for power_v in range(degree + 1)]


def gauss_taps():
    positions = np.arange(-HALO, HALO + 1).astype(np.float32)
    stacked = []
    for fraction in sigma_fractions:
        sigma = fraction * HALO
        values = np.exp(-positions * positions / np.float32(2.0 * sigma * sigma))
        stacked.append(values / np.sum(values))
    return np.stack(stacked).astype(ml_dtypes.bfloat16)


def across_band(taps):
    band = np.zeros((2 * LANES, BASES * LANES), taps.dtype)
    for b in range(BASES):
        for out in range(LANES):
            band[out : out + 2 * HALO + 1, b * LANES + out] = taps[b]
    return band


def down_band(taps):
    band = np.zeros((BASES, LANES, LANES + 2 * HALO), taps.dtype)
    for b in range(BASES):
        for out in range(LANES):
            band[b, out, out : out + 2 * HALO + 1] = taps[b]
    return band


SMEM = pl.BlockSpec(memory_space=pltpu.SMEM)
VMEM = pl.BlockSpec(memory_space=pltpu.VMEM)
ANY = pl.BlockSpec(memory_space=pl.ANY)
CHEAP = pl.CostEstimate(flops=0, bytes_accessed=0, transcendentals=0)


def split_index(index, size):
    if size & (size - 1) == 0:
        return jnp.right_shift(index, size.bit_length() - 1), jnp.bitwise_and(index, size - 1)
    return lax.div(index, size), lax.rem(index, size)


def piece_at(message, slot, block_side):
    if len(message.shape) == 3:
        return message.at[slot]
    start = slot * block_side
    if not isinstance(slot, int):
        start = pl.multiple_of(start, block_side)
    return message.at[pl.ds(start, block_side), :]


def order_kernel(cols_total, owner_ref, offset_ref, pieces_ref, template_ref, *refs):
    outs = refs[:-10]
    near_ref, far_ref, label_ref, held, edges, given, meta, order_v, order_s, sems = refs[-10:]
    count = held.shape[0]
    fetch = pltpu.make_async_copy(pieces_ref, held, sems.at[len(outs)])
    tables = [
        pltpu.make_async_copy(owner_ref, given.at[0], sems.at[len(outs) + 4]),
        pltpu.make_async_copy(offset_ref, given.at[1], sems.at[len(outs) + 5]),
    ]
    for table in tables:
        table.start()
    fetch.start()
    side = edges.shape[1]
    rims = [
        pltpu.make_async_copy(template_ref.at[:, :LANES], edges.at[0], sems.at[len(outs) + 2]),
        pltpu.make_async_copy(template_ref.at[:, side - LANES :], edges.at[1], sems.at[len(outs) + 3]),
    ]
    for rim in rims:
        rim.start()
    my_row, my_col = lax.axis_index("py"), lax.axis_index("px")
    even_col = jnp.bitwise_and(my_col, 1) == 0
    near = 1 - 2 * jnp.bitwise_and(my_col, 1)
    core = 1 - 2 * jnp.bitwise_and(my_row, 1)

    meta[...] = jnp.zeros_like(meta)
    for table in tables:
        table.wait()
    meta[0:1, :count] = given[0]
    meta[1:2, :count] = given[1]
    lane = lax.broadcasted_iota(jnp.int32, (1, LANES), 1)
    row, col = split_index(meta[0:1, :], cols_total)
    dy, dx = row - my_row, col - my_col
    flat = dy == 0
    to_core = dy == core
    kind = jnp.where(
        dx == 0,
        jnp.where(flat, 4, jnp.where(to_core, 5, 6)),
        jnp.where(
            dx == near,
            jnp.where(flat, 3, jnp.where(to_core, 8, 7)),
            jnp.where(flat, 2, jnp.where(to_core, 1, 0)),
        ),
    )
    kind = jnp.where(lane < count, kind, 9)
    packed = (3 * (dy + 1) + dx + 2) * 256 + meta[1:2, :]

    def both(line):
        across = jnp.broadcast_to(line.astype(jnp.float32), (LANES, LANES))
        return across, across.T

    kind_l, kind_s = both(kind)
    _, packed_s = both(packed)
    sub = lax.broadcasted_iota(jnp.int32, (LANES, LANES), 0)
    lan = lax.broadcasted_iota(jnp.int32, (LANES, LANES), 1)

    def total(flags):
        return jnp.sum(jnp.where(flags, 1.0, 0.0), axis=1, keepdims=True)

    rank = total((kind_l == kind_s) & (lan < sub))
    mine = kind_s[:, 0:1]
    before = total((kind_l < kind_s) & ((kind_l >= 7.0) | (kind_s < 7.0)))
    slot = jnp.where(mine < 7.0, before + rank, jnp.where(mine < 9.0, (count - 1.0) - before - rank, -1.0))
    extra = jnp.where(
        mine == 5.0, count + rank, jnp.where(mine == 6.0, (count + CAP) + rank, -1.0)
    )
    place = lan.astype(jnp.float32)
    here = (place == slot) | (place == extra)
    order = jnp.sum(jnp.where(here, sub.astype(jnp.float32), 0.0), axis=0, keepdims=True)
    labels = jnp.sum(jnp.where(here, packed_s, 0.0), axis=0, keepdims=True)
    order_v[...] = jnp.broadcast_to(order, order_v.shape).astype(jnp.int32)
    to_smem = pltpu.make_async_copy(order_v, order_s, sems.at[len(outs) + 1])
    to_smem.start()
    labels = labels.astype(jnp.int32)
    which = lax.broadcasted_iota(jnp.int32, label_ref.shape, 0)
    label_rows = jnp.where(
        which == 0, jnp.right_shift(labels, 8), jnp.where(which == 1, jnp.bitwise_and(labels, 255), 0)
    ).astype(jnp.float32).astype(jnp.bfloat16)
    label_ref[...] = label_rows
    near_ref[:, side:] = label_rows
    far_ref[:, side:] = label_rows
    to_smem.wait()
    fetch.wait()
    for index, out_ref in enumerate(outs):
        for slot_at in range(CAP):
            pltpu.make_async_copy(
                held.at[order_s[0, index * CAP + slot_at]], piece_at(out_ref, slot_at, held.shape[1]), sems.at[index]
            ).start()
    for rim in rims:
        rim.wait()
    for block in range(side // LANES):
        rows = slice(block * LANES, (block + 1) * LANES)
        left = edges[0, rows, :].astype(jnp.float32).T[:HALO]
        right = edges[1, rows, :].astype(jnp.float32).T[LANES - HALO :]
        near_ref[:, rows] = jnp.where(even_col, right, left).astype(near_ref.dtype)
        far_ref[:, rows] = jnp.where(even_col, left, right).astype(far_ref.dtype)
    for index, out_ref in enumerate(outs):
        pltpu.make_async_copy(outs[0], outs[0], sems.at[index]).wait()


def order_pieces(owner_map, offsets, pieces, template, cols_total):
    count, block_side, _ = pieces.shape
    side = template.shape[0]
    parts = count // CAP + 2
    chunk = jax.ShapeDtypeStruct((CAP, block_side, block_side), pieces.dtype)
    mail = jax.ShapeDtypeStruct((2 * CAP, block_side, block_side), pieces.dtype)
    rim = jax.ShapeDtypeStruct((HALO, side + LANES), template.dtype)
    *outs, near, far, labels = pl.pallas_call(
        functools.partial(order_kernel, cols_total),
        out_shape=(chunk,) * (parts - 2)
        + (mail, mail)
        + (rim, rim, jax.ShapeDtypeStruct((HALO, LANES), template.dtype)),
        in_specs=[ANY, ANY, ANY, ANY],
        out_specs=(ANY,) * parts + (VMEM,) * 3,
        scratch_shapes=[
            pltpu.VMEM(pieces.shape, pieces.dtype),
            pltpu.VMEM((2, side, LANES), template.dtype),
            pltpu.VMEM((2, 1, count), jnp.int32),
            pltpu.VMEM((8, LANES), jnp.int32),
            pltpu.VMEM((8, LANES), jnp.int32),
            pltpu.SMEM((8, LANES), jnp.int32),
            pltpu.SemaphoreType.DMA((parts + 6,)),
        ],
        compiler_params=pltpu.CompilerParams(vmem_limit_bytes=58 << 20),
        cost_estimate=CHEAP,
        name="order_pieces",
    )(owner_map.reshape(1, -1), offsets.reshape(1, -1), pieces, template)
    return outs[:-2], outs[-2], outs[-1], near, far, labels


def rim_rows(side):
    return HALO * (side // LANES + 3)


def row_rims_kernel(
    template_ref, near_ref, far_ref, label_ref, core_out, other_out, edges, packed, sems
):
    side = edges.shape[2]
    tiles = side // LANES
    fetches = [
        pltpu.make_async_copy(template_ref.at[:HALO, :], edges.at[0], sems.at[0]),
        pltpu.make_async_copy(template_ref.at[side - HALO :, :], edges.at[1], sems.at[1]),
    ]
    for fetch in fetches:
        fetch.start()
    even_row = jnp.bitwise_and(lax.axis_index("py"), 1) == 0
    sub = lax.broadcasted_iota(jnp.int32, (HALO, LANES), 0)
    own = label_ref[...].astype(jnp.float32)
    near = near_ref[:, side:].astype(jnp.float32)
    far = far_ref[:, side:].astype(jnp.float32)
    pairs = own
    for index, table in ((1, near), (2, far)):
        for row in (0, 1):
            pairs = jnp.where(sub == 2 * index + row, table[row : row + 1, :], pairs)
    pairs = pairs.astype(label_ref.dtype)
    corners = []
    for strip in (near_ref, far_ref):
        low = strip[:, side - LANES : side].astype(jnp.float32)
        low = jnp.concatenate([low[:, LANES - HALO :], low[:, : LANES - HALO]], axis=1).astype(strip.dtype)
        corners.append((strip[:, :LANES], low))
    for fetch in fetches:
        fetch.wait()
    stores = []
    for index, (out_ref, upper) in enumerate(((core_out, jnp.logical_not(even_row)), (other_out, even_row))):
        for tile in range(tiles):
            cols = slice(tile * LANES, (tile + 1) * LANES)
            packed[index, tile * HALO : (tile + 1) * HALO, :] = jnp.where(upper, edges[0, :, cols], edges[1, :, cols])
        for corner, (top, low) in enumerate(corners):
            start = (tiles + corner) * HALO
            packed[index, start : start + HALO, :] = jnp.where(upper, top, low)
        packed[index, (tiles + 2) * HALO :, :] = pairs
        rows = out_ref.shape[0]
        stores.append(
            pltpu.make_async_copy(
                packed.at[index], out_ref.at[rows - packed.shape[1] : rows, :], sems.at[2 + index]
            )
        )
        stores[-1].start()
    for store in stores:
        store.wait()


def row_rims(template, near, far, labels):
    side = template.shape[0]
    message = jax.ShapeDtypeStruct((rim_rows(side), LANES), template.dtype)
    return pl.pallas_call(
        row_rims_kernel,
        out_shape=(message, message),
        in_specs=[ANY, VMEM, VMEM, VMEM],
        out_specs=(ANY, ANY),
        scratch_shapes=[
            pltpu.VMEM((2, HALO, side), template.dtype),
            pltpu.VMEM((2, rim_rows(side), LANES), template.dtype),
            pltpu.SemaphoreType.DMA((4,)),
        ],
        compiler_params=pltpu.CompilerParams(vmem_limit_bytes=6 << 20),
        cost_estimate=CHEAP,
        name="row_rims",
    )(template, near, far, labels)


def forward_kernel(part_ref, core_in, other_in, core_out, other_out, sems):
    count = part_ref.shape[0]
    stores = [
        pltpu.make_async_copy(part_ref, out_ref.at[pl.ds(count, count)], sems.at[index])
        for index, out_ref in enumerate((core_out, other_out))
    ]
    for store in stores:
        store.start()
    for store in stores:
        store.wait()


def add_forwarded(part, to_core, to_other):
    message = jax.ShapeDtypeStruct(to_core.shape, to_core.dtype)
    return pl.pallas_call(
        forward_kernel,
        out_shape=(message, message),
        in_specs=[VMEM, ANY, ANY],
        out_specs=(ANY, ANY),
        scratch_shapes=[pltpu.SemaphoreType.DMA((2,))],
        input_output_aliases={1: 0, 2: 1},
        compiler_params=pltpu.CompilerParams(vmem_limit_bytes=6 << 20),
        cost_estimate=CHEAP,
        name="forward_pieces",
    )(part, to_core, to_other)


def fill_tables(even_row, even_col, own_ref, core_ref, other_ref, blocks_ref, share_ref):
    near_step = jnp.where(even_col, 1, -1)
    core_step = jnp.where(even_row, 1, -1)
    sub = lax.broadcasted_iota(jnp.int32, (LANES, LANES), 0)
    lane = lax.broadcasted_iota(jnp.int32, (LANES, LANES), 1)
    table = jnp.full((LANES, LANES), -1.0, jnp.float32)
    for group, (ref, row_step) in enumerate(((own_ref, 0), (core_ref, core_step), (other_ref, -core_step))):
        rows = ref[ref.shape[0] - HALO :, :].astype(jnp.float32)
        for index, col_step in enumerate((0, near_step, -near_step)):
            wanted = (5 - 3 * row_step - col_step) * jnp.int32(1)
            match = rows[2 * index : 2 * index + 1, :] == wanted.astype(jnp.float32)
            line = jnp.where(match, rows[2 * index + 1 : 2 * index + 2, :], -1.0)
            table = jnp.where(sub == 3 * group + index, line, table)
    blocks_ref[...] = table[: blocks_ref.shape[0]].astype(jnp.int32)
    upright = table.T
    counts = jnp.zeros((1, LANES), jnp.float32)
    for source in range(9):
        column = upright[: LANES // 2, source : source + 1]
        counts = counts + jnp.sum(
            jnp.where(column == lane[: LANES // 2].astype(jnp.float32), 1.0, 0.0), axis=0, keepdims=True
        )
    share_ref[...] = jnp.broadcast_to(1.0 / jnp.maximum(counts, 1.0), share_ref.shape)


def weight_rows(coef_ref, start, width, side, cols_total, my_col):
    col = lax.broadcasted_iota(jnp.int32, (1, width), 1) + (start + my_col * side)
    u = (col.astype(jnp.float32) + 0.5) * (2.0 / (side * cols_total)) - 1.0
    powers = [jnp.ones_like(u)]
    for _ in range(DEGREE):
        powers.append(powers[-1] * u)
    rows = []
    for b in range(BASES):
        for j in range(DEGREE + 1):
            total = jnp.zeros_like(u)
            for i in range(DEGREE + 1 - j):
                total = total + coef_ref[b, term_powers.index((i, j))] * powers[i]
            rows.append(total)
    return rows


def minus_weighted(smoothed, polys, cols, start, side, rows_total, my_row):
    shape = smoothed[0].shape
    row = lax.broadcasted_iota(jnp.int32, shape, 0) + (start + my_row * side)
    v = (row.astype(jnp.float32) + 0.5) * (2.0 / (side * rows_total)) - 1.0
    total = jnp.zeros(shape, jnp.float32)
    for b in range(BASES):
        power = b * (DEGREE + 1)
        weight = polys[power + DEGREE : power + DEGREE + 1, cols] * v
        for j in range(DEGREE - 1, 0, -1):
            weight = (weight + polys[power + j : power + j + 1, cols]) * v
        weight = weight + polys[power : power + 1, cols]
        total = total - weight * smoothed[b]
    return total


def interior_kernel(
    extent, coef_ref, centre_ref, across_ref, down_ref, out_ref, sides_ref, ends_ref,
    padded, across, polys, ready, sems,
):
    side = centre_ref.shape[0]
    rows_total, cols_total = extent
    inner = side - 2 * LANES
    copies = [
        pltpu.make_async_copy(centre_ref.at[:, : 2 * LANES], sides_ref.at[0], sems.at[2]),
        pltpu.make_async_copy(centre_ref.at[:, side - 2 * LANES :], sides_ref.at[1], sems.at[3]),
        pltpu.make_async_copy(centre_ref.at[: 2 * HALO, :], ends_ref.at[0], sems.at[4]),
        pltpu.make_async_copy(centre_ref.at[side - 2 * HALO :, :], ends_ref.at[1], sems.at[5]),
    ]
    for copy in copies:
        copy.start()
    reach = inner + LANES
    padded[:, :reach] = centre_ref[:, LANES - HALO : LANES - HALO + reach]
    for index, line in enumerate(weight_rows(coef_ref, LANES, inner, side, cols_total, lax.axis_index("px"))):
        polys[index : index + 1, :] = line
    for b in range(BASES):
        across[b, :HALO, :] = jnp.zeros((HALO, inner), across.dtype)
        across[b, HALO + side :, :] = jnp.zeros((HALO, inner), across.dtype)

    tall = side // 2
    for start in (0, tall):
        for j in range(inner // LANES):
            window = padded[start : start + tall, j * LANES : (j + 2) * LANES]
            summed = jnp.dot(window, across_ref[...], preferred_element_type=jnp.float32)
            for b in range(BASES):
                across[b, HALO + start : HALO + start + tall, j * LANES : (j + 1) * LANES] = summed[
                    :, b * LANES : (b + 1) * LANES
                ].astype(across.dtype)

    wide = 256

    def send(start, slot):
        return pltpu.make_async_copy(
            ready.at[slot], out_ref.at[pl.ds(start, LANES), LANES : LANES + inner], sems.at[slot]
        )

    def down_step(step, carry):
        start = pl.multiple_of(step * LANES, LANES)
        slot = jnp.bitwise_and(step, 1)

        @pl.when(step >= 2)
        def _():
            send(start, slot).wait()

        for n in range(inner // wide):
            cols = slice(n * wide, (n + 1) * wide)
            smoothed = [
                jnp.dot(
                    down_ref[b], across[b, pl.ds(start, LANES + 2 * HALO), cols], preferred_element_type=jnp.float32
                )
                for b in range(BASES)
            ]
            ready[slot, :, cols] = minus_weighted(smoothed, polys, cols, start, side, rows_total, lax.axis_index("py"))
        send(start, slot).start()
        return carry

    lax.fori_loop(0, side // LANES, down_step, 0)
    for slot in (0, 1):
        send(0, slot).wait()
    for copy in copies:
        copy.wait()


def interior(extent, coefficients, centre):
    side = centre.shape[0]
    inner = side - 2 * LANES
    taps = gauss_taps()
    return pl.pallas_call(
        functools.partial(interior_kernel, extent),
        out_shape=(
            jax.ShapeDtypeStruct((side, side), jnp.float32),
            jax.ShapeDtypeStruct((2, side, 2 * LANES), centre.dtype),
            jax.ShapeDtypeStruct((2, 2 * HALO, side), centre.dtype),
        ),
        in_specs=[SMEM] + [VMEM] * 3,
        out_specs=(ANY, ANY, ANY),
        scratch_shapes=[
            pltpu.VMEM((side, inner + LANES), jnp.bfloat16),
            pltpu.VMEM((BASES, side + 2 * HALO, inner), jnp.bfloat16),
            pltpu.VMEM((16, inner), jnp.float32),
            pltpu.VMEM((2, LANES, inner), jnp.float32),
            pltpu.SemaphoreType.DMA((6,)),
        ],
        compiler_params=pltpu.CompilerParams(vmem_limit_bytes=40 << 20),
        cost_estimate=pl.CostEstimate(flops=int(8e9), bytes_accessed=1, transcendentals=0),
        name="matched_inside",
    )(coefficients, centre, jnp.asarray(across_band(taps)), jnp.asarray(down_band(taps)))


def upright(near_block, far_block, even_col):
    near_block = near_block.astype(jnp.float32)
    far_block = far_block.astype(jnp.float32)
    empty = jnp.zeros((LANES - HALO, LANES), jnp.float32)
    left = jnp.concatenate([jnp.where(even_col, far_block, near_block), empty], axis=0).T
    right = jnp.concatenate([jnp.where(even_col, near_block, far_block), empty], axis=0).T
    return left.astype(jnp.bfloat16), right.astype(jnp.bfloat16)


def sides_kernel(
    extent, coef_ref, near_ref, far_ref, across_ref, down_ref, sides, base_ref, out_ref,
    padded, across, polys, columns, sems,
):
    side = sides.shape[1]
    rows_total, cols_total = extent
    even_col = jnp.bitwise_and(lax.axis_index("px"), 1) == 0
    for start, first in ((0, 0), (side - LANES, LANES)):
        for index, line in enumerate(weight_rows(coef_ref, start, LANES, side, cols_total, lax.axis_index("px"))):
            polys[index : index + 1, first : first + LANES] = line
    for b in range(BASES):
        across[b, :HALO, :] = jnp.zeros((HALO, 2 * LANES), across.dtype)
        across[b, HALO + side :, :] = jnp.zeros((HALO, 2 * LANES), across.dtype)
    for block in range(side // LANES):
        rows = slice(block * LANES, (block + 1) * LANES)
        left, right = upright(near_ref[:, rows], far_ref[:, rows], even_col)
        padded[0, rows, :HALO] = left[:, :HALO]
        padded[1, rows, LANES + HALO :] = right[:, : LANES - HALO]
    padded[0, :, HALO:] = sides[0, :, : 2 * LANES - HALO]
    padded[1, :, : LANES + HALO] = sides[1, :, LANES - HALO :]

    tall = side // 2
    for end in (0, 1):
        for start in (0, tall):
            summed = jnp.dot(padded[end, start : start + tall, :], across_ref[...], preferred_element_type=jnp.float32)
            for b in range(BASES):
                across[b, HALO + start : HALO + start + tall, end * LANES : (end + 1) * LANES] = summed[
                    :, b * LANES : (b + 1) * LANES
                ].astype(across.dtype)
    both = slice(0, 2 * LANES)

    def send(rows, end):
        return pltpu.make_async_copy(
            columns.at[rows, pl.ds(end * LANES, LANES)],
            out_ref.at[rows, pl.ds(end * (side - LANES), LANES)],
            sems.at[end],
        )

    def down_step(step, carry):
        start = pl.multiple_of(step * LANES, LANES)
        smoothed = [
            jnp.dot(down_ref[b], across[b, pl.ds(start, LANES + 2 * HALO), :], preferred_element_type=jnp.float32)
            for b in range(BASES)
        ]
        rows = pl.ds(start, LANES)
        columns[rows, :] = minus_weighted(
            smoothed, polys, both, start, side, rows_total, lax.axis_index("py")
        )
        for end in (0, 1):
            send(rows, end).start()
        return carry

    lax.fori_loop(0, side // LANES, down_step, 0)
    for end in (0, 1):
        send(pl.ds(0, side), end).wait()


def matched_sides(extent, base, coefficients, sides, near, far):
    side = sides.shape[1]
    taps = gauss_taps()
    return pl.pallas_call(
        functools.partial(sides_kernel, extent),
        out_shape=jax.ShapeDtypeStruct((side, side), jnp.float32),
        in_specs=[SMEM, VMEM, VMEM, VMEM, VMEM, VMEM, ANY],
        out_specs=ANY,
        scratch_shapes=[
            pltpu.VMEM((2, side, 2 * LANES), jnp.bfloat16),
            pltpu.VMEM((BASES, side + 2 * HALO, 2 * LANES), jnp.bfloat16),
            pltpu.VMEM((16, 2 * LANES), jnp.float32),
            pltpu.VMEM((side, 2 * LANES), jnp.float32),
            pltpu.SemaphoreType.DMA((2,)),
        ],
        input_output_aliases={6: 0},
        compiler_params=pltpu.CompilerParams(vmem_limit_bytes=16 << 20),
        cost_estimate=CHEAP,
        name="matched_sides",
    )(
        coefficients, near, far, jnp.asarray(across_band(taps)), jnp.asarray(down_band(taps)), sides, base
    )


def ends_kernel(
    extent, coef_ref, near_ref, far_ref, core_ref, other_ref, sent_ref, across_ref, down_ref, ends,
    base_ref, out_ref, blocks_ref, share_ref, window, polys, lines, sems,
):
    side = ends.shape[2]
    rows_total, cols_total = extent
    deep = 3 * HALO
    tiles = side // LANES
    even_row = jnp.bitwise_and(lax.axis_index("py"), 1) == 0
    even_col = jnp.bitwise_and(lax.axis_index("px"), 1) == 0
    fill_tables(even_row, even_col, sent_ref, core_ref, other_ref, blocks_ref, share_ref)
    for index, line in enumerate(weight_rows(coef_ref, 0, side, side, cols_total, lax.axis_index("px"))):
        polys[index : index + 1, :] = line
    window[...] = jnp.zeros_like(window)
    core_rim, other_rim = core_ref[...], other_ref[...]
    near_corner = slice(tiles * HALO, (tiles + 1) * HALO)
    far_corner = slice((tiles + 1) * HALO, (tiles + 2) * HALO)
    centre = slice(HALO, HALO + side)
    right_cols = slice(HALO + side, side + LANES)
    for end, upper in ((0, even_row), (1, jnp.logical_not(even_row))):
        rim = jnp.where(upper, other_rim, core_rim)
        first = end * deep
        outer = first + (2 * HALO if end else 0)
        inner = first + (0 if end else HALO)
        left, right = upright(rim[near_corner], rim[far_corner], even_col)
        window[outer : outer + HALO, :HALO] = left[:HALO, :HALO]
        window[outer : outer + HALO, right_cols] = right[:HALO, : LANES - HALO]
        window[outer : outer + HALO, centre] = jnp.concatenate(
            [rim[tile * HALO : (tile + 1) * HALO] for tile in range(tiles)], axis=1
        )
        cols = slice(side - LANES, side) if end else slice(0, LANES)
        left, right = upright(near_ref[:, cols], far_ref[:, cols], even_col)
        rows = slice(LANES - 2 * HALO, LANES) if end else slice(0, 2 * HALO)
        window[inner : inner + 2 * HALO, :HALO] = left[rows, :HALO]
        window[inner : inner + 2 * HALO, right_cols] = right[rows, : LANES - HALO]
    for end in (0, 1):
        inner = end * deep + (0 if end else HALO)
        window[inner : inner + 2 * HALO, centre] = ends[end]

    parts = [[] for _ in range(BASES)]
    for j in range(tiles):
        summed = jnp.dot(
            window[:, j * LANES : (j + 2) * LANES], across_ref[...], preferred_element_type=jnp.float32
        )
        for b in range(BASES):
            parts[b].append(summed[:, b * LANES : (b + 1) * LANES].astype(ends.dtype))
    across = [jnp.concatenate(part, axis=1) for part in parts]
    stores = []
    for end in (0, 1):
        smoothed = [
            jnp.dot(
                down_ref[b, :HALO, :deep], across[b][end * deep : (end + 1) * deep], preferred_element_type=jnp.float32
            )
            for b in range(BASES)
        ]
        start = end * (side - HALO)
        lines[end] = minus_weighted(smoothed, polys, slice(0, side), start, side, rows_total, lax.axis_index("py"))
        stores.append(pltpu.make_async_copy(lines.at[end], out_ref.at[start : start + HALO, :], sems.at[end]))
        stores[-1].start()
    for store in stores:
        store.wait()


def matched_ends(extent, base, sent, coefficients, ends, near, far, core, other):
    side = ends.shape[2]
    taps = gauss_taps()
    return pl.pallas_call(
        functools.partial(ends_kernel, extent),
        out_shape=(
            jax.ShapeDtypeStruct((side, side), jnp.float32),
            jax.ShapeDtypeStruct((HALO, LANES), jnp.int32),
            jax.ShapeDtypeStruct((8, LANES), jnp.float32),
        ),
        in_specs=[SMEM] + [VMEM] * 8 + [ANY],
        out_specs=(ANY, VMEM, VMEM),
        scratch_shapes=[
            pltpu.VMEM((6 * HALO, side + LANES), jnp.bfloat16),
            pltpu.VMEM((16, side), jnp.float32),
            pltpu.VMEM((2, HALO, side), jnp.float32),
            pltpu.SemaphoreType.DMA((2,)),
        ],
        input_output_aliases={9: 0},
        compiler_params=pltpu.CompilerParams(vmem_limit_bytes=10 << 20),
        cost_estimate=CHEAP,
        name="matched_ends",
    )(
        coefficients, near, far, core, other, sent,
        jnp.asarray(across_band(taps)), jnp.asarray(down_band(taps)), ends, base,
    )


def add_kernel(plan, blocks_side, blocks_ref, share_ref, base_ref, *refs):
    count = len(plan)
    messages = refs[:count]
    out_ref, held, hits, slots, left, seen, sems = refs[count:]
    block_side = held.shape[0] // blocks_side

    def area(block):
        row, col = split_index(block, blocks_side)
        rows = pl.ds(pl.multiple_of(row * block_side, block_side), block_side)
        cols = pl.ds(pl.multiple_of(col * block_side, block_side), block_side)
        return rows, cols

    for block in range(blocks_side * blocks_side):
        left[block] = 0
        seen[block] = 0

    found = jnp.int32(0)
    ends = []
    for source, first, skipped in plan:
        for slot in range(CAP):
            block = blocks_ref[source, first + slot]
            hits[found] = block
            slots[found] = skipped + slot
            found = found + jnp.where(block >= 0, 1, 0)
        ends.append(found)

    def fetch_base(block):
        rows, cols = area(block)
        return pltpu.make_async_copy(base_ref.at[rows, cols], held.at[rows, cols], sems.at[block])

    def store_base(block):
        rows, cols = area(block)
        return pltpu.make_async_copy(held.at[rows, cols], out_ref.at[rows, cols], sems.at[block])

    def begin(index, carry):
        block = hits[index]
        left[block] = left[block] + 1

        @pl.when(seen[block] == 0)
        def _():
            fetch_base(block).start()
            seen[block] = 1

        return carry

    lax.fori_loop(0, found, begin, 0)

    start = jnp.int32(0)
    for message, end in zip(messages, ends):

        def add(index, carry, message=message):
            block = hits[index]
            rows, cols = area(block)

            @pl.when(seen[block] == 1)
            def _():
                fetch_base(block).wait()
                seen[block] = 2

            held[rows, cols] = held[rows, cols] + message[slots[index]].astype(jnp.float32) * share_ref[0, block]
            more = left[block] - 1
            left[block] = more

            @pl.when(more == 0)
            def _():
                store_base(block).start()

            return carry

        lax.fori_loop(start, end, add, 0)
        start = end

    def finish(index, carry):
        block = hits[index]

        @pl.when(seen[block] == 2)
        def _():
            store_base(block).wait()
            seen[block] = 3

        return carry

    lax.fori_loop(0, found, finish, 0)


def add_pieces(name, base, blocks, shares, messages, blocks_side, cost):
    side = base.shape[0]
    plan = tuple((source, first, sum(skipped)) for _, source, first, *skipped in messages)
    arrays = [message[0] for message in messages]
    room = CAP * len({source for source, _, _ in plan}) + 8
    per_tile = blocks_side * blocks_side
    return pl.pallas_call(
        functools.partial(add_kernel, plan, blocks_side),
        out_shape=jax.ShapeDtypeStruct(base.shape, base.dtype),
        in_specs=[SMEM, SMEM, ANY] + [VMEM] * len(arrays),
        out_specs=ANY,
        scratch_shapes=[
            pltpu.VMEM((side, side), jnp.float32),
            pltpu.SMEM((room,), jnp.int32),
            pltpu.SMEM((room,), jnp.int32),
            pltpu.SMEM((per_tile,), jnp.int32),
            pltpu.SMEM((per_tile,), jnp.int32),
            pltpu.SemaphoreType.DMA((per_tile,)),
        ],
        input_output_aliases={2: 0},
        compiler_params=pltpu.CompilerParams(vmem_limit_bytes=16 << 20),
        cost_estimate=pl.CostEstimate(flops=int(cost * 1e9), bytes_accessed=0, transcendentals=0),
        name=name,
    )(blocks, shares, base, *arrays)


class Grid:
    def __init__(self, rows, cols):
        self.rows, self.cols = rows, cols

    def pairs(self, target):
        found = []
        for row in range(self.rows):
            for col in range(self.cols):
                to_row, to_col = target(row, col)
                if 0 <= to_row < self.rows and 0 <= to_col < self.cols:
                    found.append((row * self.cols + col, to_row * self.cols + to_col))
        return found

    def near(self, array):
        return lax.ppermute(array, ("py", "px"), self.pairs(lambda r, c: (r, c ^ 1)))

    def far(self, array):
        return lax.ppermute(array, ("py", "px"), self.pairs(lambda r, c: (r, c + 1 if c % 2 else c - 1)))

    def beyond(self, array):
        return lax.ppermute(array, ("py", "px"), self.pairs(lambda r, c: (r, c - 2 if c % 2 else c + 2)))

    def core(self, array):
        return lax.ppermute(array, ("py", "px"), self.pairs(lambda r, c: (r ^ 1, c)))

    def other(self, array):
        return lax.ppermute(array, ("py", "px"), self.pairs(lambda r, c: (r + 1 if r % 2 else r - 1, c)))


def on_device(pieces, owner_map, offsets, template, coefficients):
    bar = lax.optimization_barrier
    rows_total = lax.axis_size("py")
    cols_total = lax.axis_size("px")
    grid = Grid(rows_total, cols_total)
    count, block_side, _ = pieces.shape
    side = template.shape[0]
    blocks_side = side // block_side

    chunks, own_core, own_other, near_rim, far_rim, labels = order_pieces(
        owner_map, offsets, pieces, template, cols_total
    )

    near_strip = grid.near(near_rim)
    far_strip = grid.far(far_rim)
    x0, x1, x2, x3 = [grid.near(chunk) for chunk in chunks]
    extent = (rows_total, cols_total)
    template, labels = bar((template, labels))
    base, sides, ends = interior(extent, coefficients, template)
    x0, near_strip, far_strip, base = bar((x0, near_strip, far_strip, base))
    z0 = grid.beyond(x0)
    to_core, to_other = row_rims(template, near_strip, far_strip, labels)
    other_rows, core_rows = grid.other(to_other), grid.core(to_core)
    x1, core_rows, other_rows, base = bar((x1, core_rows, other_rows, base))
    z1 = grid.beyond(x1)
    base = matched_sides(extent, base, coefficients, sides, near_strip, far_strip)

    own, near, far = 0, 1, 2
    core, other = 3, 6

    z0, base = bar((z0, base))
    own_core, own_other = add_forwarded(z0, own_core, own_other)
    from_core, from_other = grid.core(own_core), grid.other(own_other)
    x2, base = bar((x2, base))
    z2 = grid.beyond(x2)
    base, blocks, shares = matched_ends(
        extent, base, to_core, coefficients, ends, near_strip, far_strip, core_rows, other_rows
    )

    z1, base = bar((z1, base))
    early = [(chunk, own, i * CAP) for i, chunk in enumerate(chunks)]
    early += [(x0, near, 0), (x1, near, CAP), (x2, near, 2 * CAP), (z0, far, 0), (z1, far, CAP)]
    base = add_pieces("add_early", base, blocks, shares, early, blocks_side, 0)

    x3, base = bar((x3, base))
    vx3 = (grid.core(jnp.concatenate([z1, x2, x3], axis=0)), grid.other(x3))
    late = [(x3, near, 3 * CAP), (z2, far, 2 * CAP)]
    late += [(from_core, core, count), (from_other, other, count + CAP)]
    late += [(from_core, core + far, 0, CAP), (from_other, other + far, 0, CAP)]
    base = add_pieces("add_late", base, blocks, shares, late, blocks_side, 12)
    last = [(vx3[0], core + far, CAP), (vx3[0], core + near, 2 * CAP, CAP)]
    last += [(vx3[0], core + near, 3 * CAP, 2 * CAP), (vx3[1], other + near, 3 * CAP)]
    return add_pieces("add_last", base, blocks, shares, last, blocks_side, 12)


def solution(mesh):
    in_specs = (P(("py", "px"), None, None), P(("py", "px")), P(("py", "px")), P("py", "px"), P())
    out_specs = P("py", "px")
    return jax.shard_map(on_device, mesh=mesh, in_specs=in_specs, out_specs=out_specs, check_vma=False)
```
